256 devices in a mesh: facet: 16 (over z, x_hi), strip: 16 (over x_lo, y, core).
Axes of the slice: x: 4 (x_hi: 2, x_lo: 2; x = x_hi * 2 + x_lo), y: 4, z: 8, core: 2. Of those that a mesh axis runs over, the one named last changes fastest.
Arguments:
- facets: bfloat16 [16, 2, 512, 8192], P('facet', None, None, 'strip'), may hold values from -6 to 6
- offsets: int32 [4], replicated, may hold values from 0 to 32767
- visibilities: float32 [2, 512, 2048], P(None, 'strip', 'facet'), may hold values from -24 to 24
- weights: float32 [512, 2048], P('strip', 'facet'), may hold values from 0.1 to 1
- mask: int32 [512, 2048], P('strip', 'facet'), may hold values 0 or 1
Outputs:
- facet_update: bfloat16 [16, 2, 512, 8192], P('facet', None, None, 'strip')
The draws below stay inside these ranges and needn't reach their ends.
Inputs may be any that keep to these rules, and one draw needn't show every extreme that they name: `mask`: 1 where the cell holds a sampled visibility.
All inputs are finite; a program needn't handle non-finite values. No bound on the sum of `mask` on one device may be relied on, other than what follows from the above.
Results may differ from the reference program's by a relative error of at most 0.0058.
Values may be sent and summed in bfloat16 or wider, within the bound.
A program may use at most 128 MiB of HBM per device.

```python
import math
import jax
import jax.numpy as jnp
from jax import lax

NG = 32768
XM = 8192
SG = 512
NSUB = 4
FROWS = 4
NF = 16
NK = 2048


def place_ends(drawn, stream_key, low, largest):
    dims = drawn.shape
    index_at = [jax.random.randint(jax.random.fold_in(stream_key, axis), (), 0, dims[axis]) for axis in range(len(dims))]
    drawn = drawn.at[tuple(index_at)].set(low)
    longest = dims.index(max(dims))
    index_at[longest] = (index_at[longest] + 1) % dims[longest]
    return drawn.at[tuple(index_at)].set(largest)


def block_scale(own_key, dims, cuts, low, largest):
    gain, own = 1.0, jax.random.fold_in(own_key, 6)
    for position, shards_of in cuts:
        heights = jnp.exp(jax.random.uniform(jax.random.fold_in(own, position), (shards_of,), jnp.float32, low / len(cuts), largest / len(cuts)))
        gain = gain * jnp.repeat(heights, dims[position] // shards_of).reshape([-1 if axis == position else 1 for axis in range(len(dims))])
    return gain


def bell_draw(stream_key, shape, deviation, limit, split=(), held_as=jnp.bfloat16):
    level = block_scale(stream_key, shape, split, -0.22, 0.18) if split else 1.0
    array = jax.random.normal(stream_key, shape, jnp.float32) * deviation * level
    return jnp.minimum(jnp.maximum(array, -limit), limit).astype(held_as)


def setup_inputs(seed: int = 0) -> dict:
    arg_keys = jax.random.split(jax.random.key(seed), 6)
    return {
        "facets": bell_draw(arg_keys[0], (NF, 2, SG, XM), 1.0, 6.0, ((0, 16), (3, 16))),
        "offsets": place_ends(jax.random.randint(arg_keys[1], (NSUB,), 0, NG), jax.random.fold_in(arg_keys[1], 1), 0, NG - 1).astype(jnp.int32),
        "visibilities": bell_draw(arg_keys[2], (2, SG, NK), 4.0, 24.0, ((1, 16), (2, 16)), jnp.float32),
        "weights": jnp.clip(jnp.exp(math.log(1.0) - 2.3025851 * jax.random.uniform(arg_keys[3], (SG, NK), jnp.float32) ** block_scale(arg_keys[3], (SG, NK), ((0, 16), (1, 16)), -0.2, 0.2)), 0.1, 1.0),
        "mask": place_ends((jax.random.randint(arg_keys[4], (SG, NK), 0, 2) < 1).astype(jnp.int32), jax.random.fold_in(arg_keys[4], 1), 0, 1),
    }


def residue_angle(count):
    return count.astype(jnp.float32) * (2.0 * math.pi / NG)

def dft_kernel(start, rows):
    positions = start + jnp.arange(rows, dtype=jnp.int32)
    cells = jnp.arange(SG, dtype=jnp.int32)
    angle = residue_angle(positions[:, None] * cells[None, :] % NG)
    return jnp.concatenate([jnp.cos(angle), jnp.sin(angle)], axis=1).astype(jnp.bfloat16)

def row_angles(start, rows, offsets):
    positions = start + jnp.arange(rows, dtype=jnp.int32)
    return residue_angle(offsets[:, None] * positions[None, :] % NG)

def column_angles(facet_index, offsets):
    centre = (facet_index % FROWS * XM + NG // 2) % NG
    cells = jnp.arange(SG, dtype=jnp.int32)
    return residue_angle((cells[None, :] * centre % NG + offsets[:, None] * centre % NG) % NG)

def forward(data, start, facet_index, offsets, kernel_table):
    columns = data.shape[1]
    rows = data.shape[2]
    phi = row_angles(start, rows, offsets)[:, None, :]
    cos_phi = jnp.cos(phi)
    sin_phi = jnp.sin(phi)
    real_part = data[0].astype(jnp.float32)[None]
    imag_part = data[1].astype(jnp.float32)[None]
    twisted = jnp.stack([real_part * cos_phi + imag_part * sin_phi, imag_part * cos_phi - real_part * sin_phi], axis=1).astype(jnp.bfloat16)
    spectra = jnp.dot(twisted.reshape(-1, rows), kernel_table, preferred_element_type=jnp.float32)
    spectra = spectra.reshape(NSUB, 2, columns, 2, SG)
    spectrum_real = spectra[:, 0, :, 0] + spectra[:, 1, :, 1]
    spectrum_imag = spectra[:, 1, :, 0] - spectra[:, 0, :, 1]
    psi = column_angles(facet_index, offsets)[:, None, :]
    cos_psi = jnp.cos(psi)
    sin_psi = jnp.sin(psi)
    scale = 1.0 / math.sqrt(XM)
    result_real = (spectrum_real * cos_psi + spectrum_imag * sin_psi) * scale
    result_imag = (spectrum_imag * cos_psi - spectrum_real * sin_psi) * scale
    stacked = jnp.stack([result_real, result_imag])
    return stacked.transpose(0, 2, 1, 3).reshape(2, columns, NSUB * SG)

def adjoint(residual, start, facet_index, offsets, kernel_table):
    columns = residual.shape[1]
    rows = kernel_table.shape[0]
    values = residual.astype(jnp.float32).reshape(2, columns, NSUB, SG).transpose(0, 2, 1, 3)
    psi = column_angles(facet_index, offsets)[:, None, :]
    cos_psi = jnp.cos(psi)
    sin_psi = jnp.sin(psi)
    first = values[0] * cos_psi - values[1] * sin_psi
    second = values[1] * cos_psi + values[0] * sin_psi
    untwisted = jnp.stack([first, second], axis=1).astype(jnp.bfloat16)
    images = jnp.einsum('mj,xpj->pmx', untwisted.reshape(-1, SG).astype(jnp.float32), kernel_table.reshape(rows, 2, SG).astype(jnp.float32))
    images = images.reshape(2, NSUB, 2, columns, rows)
    image_real = images[0, :, 0] - images[1, :, 1]
    image_imag = images[0, :, 1] + images[1, :, 0]
    phi = row_angles(start, rows, offsets)[:, None, :]
    cos_phi = jnp.cos(phi)
    sin_phi = jnp.sin(phi)
    scale = 1.0 / math.sqrt(XM)
    total_real = lax.optimization_barrier(jnp.sum(image_real * cos_phi - image_imag * sin_phi, axis=0)) * scale
    total_imag = lax.optimization_barrier(jnp.sum(image_imag * cos_phi + image_real * sin_phi, axis=0)) * scale
    return jnp.stack([total_real, total_imag])

def reference(facets, offsets, visibilities, weights, mask):
    kernel_table = dft_kernel(0, XM)
    facet_ids = jnp.arange(NF, dtype=jnp.int32)

    def one_facet(carry, item):
        index, data = item
        return (carry + forward(data, 0, index, offsets, kernel_table), None)
    model, _ = lax.scan(one_facet, jnp.zeros((2, SG, NSUB * SG), jnp.float32), (facet_ids, facets))
    factor = weights * mask.astype(jnp.float32)
    residual = (factor[None] * (visibilities - model)).astype(jnp.bfloat16)

    def back_facet(index):
        return adjoint(residual, 0, index, offsets, kernel_table).astype(jnp.bfloat16)
    return lax.map(back_facet, facet_ids)
```

```python
import functools
import math

import jax
import jax.numpy as jnp
from jax import lax
from jax.experimental import pallas as pl
from jax.experimental.pallas import tpu as pltpu
from jax.sharding import PartitionSpec as P

NSUB = 4
FROWS = 4
MESH = pl.DeviceIdType.MESH


def turn(count, cells):
    quarter = cells // 4
    shift = quarter.bit_length() - 1
    quadrant = (count + quarter // 2) >> shift
    angle = (count - (quadrant << shift)).astype(jnp.float32) * (2.0 * math.pi / cells)
    square = angle * angle
    sine = angle * (1.0 + square * (-1.0 / 6 + square * (1.0 / 120 + square * (-1.0 / 5040 + square * (1.0 / 362880)))))
    cosine = 1.0 + square * (-0.5 + square * (1.0 / 24 + square * (-1.0 / 720 + square * (1.0 / 40320))))
    odd = (quadrant & 1) == 1
    first = jnp.where(odd, sine, cosine)
    second = jnp.where(odd, cosine, sine)
    cos_value = jnp.where(((quadrant + 1) & 2) == 2, -first, first)
    sin_value = jnp.where((quadrant & 2) == 2, -second, second)
    return cos_value, sin_value


def quarter_turn(count):
    part = count & 3
    sign = jnp.where(part >= 2, -1.0, 1.0)
    even = (part & 1) == 0
    return jnp.where(even, sign, 0.0), jnp.where(even, 0.0, sign)


def kernel(
    nf, ns,
    facets, offsets, vis, weights, mask, out,
    parts, table, phase, lhs, acc, factor, vis_here, factor_here, partial, partials, resid, result,
    a_send, a_recv, v_send, v_recv, c_send, c_recv, e_send, e_recv, g_send, g_recv, local_sem,
):
    f = lax.axis_index("facet")
    t = lax.axis_index("strip")
    cols, rows = parts.shape[2], parts.shape[3]
    cells = FROWS * rows * ns
    half = table.shape[1] // 2
    chunk = partial.shape[3]
    chunks = half // chunk
    scale = 1.0 / math.sqrt(rows * ns)
    start = t * rows
    apart = f != t

    def facet_peer(i):
        return lax.rem(f + i, nf)

    def strip_peer(i):
        return lax.rem(t + i, ns)

    barrier = pltpu.get_barrier_semaphore()

    def greet_facet(i, _):
        pl.semaphore_signal(barrier, inc=1, device_id=(facet_peer(i), t), device_id_type=MESH)
        return 0

    def greet_strip(i, _):
        pl.semaphore_signal(barrier, inc=1, device_id=(f, strip_peer(i)), device_id_type=MESH)
        return 0

    lax.fori_loop(1, nf, greet_facet, 0)
    lax.fori_loop(1, ns, greet_strip, 0)

    @pl.when(apart)
    def _():
        pl.semaphore_signal(barrier, inc=1, device_id=(t, f), device_id_type=MESH)

    pl.semaphore_wait(barrier, nf + ns - 2 + apart.astype(jnp.int32))

    def facet_columns(g):
        return pl.ds(pl.multiple_of(g * cols, cols), cols)

    def send_part(peer):
        return pltpu.make_async_remote_copy(
            src_ref=facets.at[0, :, facet_columns(peer), :], dst_ref=parts.at[f],
            send_sem=a_send.at[peer], recv_sem=a_recv.at[f], device_id=(peer, t), device_id_type=MESH)

    def arrive_part(peer):
        return pltpu.make_async_remote_copy(
            src_ref=parts.at[peer], dst_ref=parts.at[peer],
            send_sem=a_send.at[peer], recv_sem=a_recv.at[peer], device_id=(peer, t), device_id_type=MESH)

    def start_part(i, _):
        send_part(facet_peer(i)).start()
        return 0

    lax.fori_loop(1, nf, start_part, 0)
    own_part = pltpu.make_async_copy(facets.at[0, :, facet_columns(f), :], parts.at[f], local_sem.at[0])
    own_part.start()

    factor[...] = weights[...] * mask[...].astype(jnp.float32)
    send_vis = pltpu.make_async_remote_copy(
        src_ref=vis, dst_ref=vis_here, send_sem=v_send.at[0], recv_sem=v_recv.at[0], device_id=(t, f), device_id_type=MESH)
    send_factor = pltpu.make_async_remote_copy(
        src_ref=factor, dst_ref=factor_here, send_sem=v_send.at[1], recv_sem=v_recv.at[1], device_id=(t, f), device_id_type=MESH)

    @pl.when(apart)
    def _():
        send_vis.start()
        send_factor.start()

    @pl.when(jnp.logical_not(apart))
    def _():
        vis_here[...] = vis[...]
        factor_here[...] = factor[...]

    with jax.named_scope("tables"):
        block = min(32, rows)

        def fill(i, _):
            base = pl.multiple_of(i * block, block)
            x = start + base + lax.broadcasted_iota(jnp.int32, (block, half), 0)
            j = lax.broadcasted_iota(jnp.int32, (block, half), 1)
            cos_value, sin_value = turn((x * j) & (cells - 1), cells)
            low = pl.ds(base, block)
            high = pl.ds(pl.multiple_of(rows + base, block), block)
            cos_value = cos_value.astype(jnp.bfloat16)
            table[low, :half] = cos_value
            table[high, half:] = cos_value
            table[low, half:] = (-sin_value).astype(jnp.bfloat16)
            table[high, :half] = sin_value.astype(jnp.bfloat16)
            return 0

        lax.fori_loop(0, rows // block, fill, 0)
        for s in range(NSUB):
            x = start + lax.broadcasted_iota(jnp.int32, (1, rows), 1)
            cos_value, sin_value = turn((x * offsets[s]) & (cells - 1), cells)
            phase[0, s] = cos_value
            phase[1, s] = sin_value

    def psi(r, s):
        j = lax.broadcasted_iota(jnp.int32, (1, half), 1)
        return quarter_turn((offsets[s] + j) * (r + 2))

    own_part.wait()

    def wait_part(i, _):
        arrive_part(facet_peer(i)).wait_recv()
        return 0

    lax.fori_loop(1, nf, wait_part, 0)

    def send_partial(peer):
        return pltpu.make_async_remote_copy(
            src_ref=partial.at[peer], dst_ref=partials.at[t],
            send_sem=c_send.at[peer], recv_sem=c_recv.at[t], device_id=(f, peer), device_id_type=MESH)

    def arrive_partial(peer):
        return pltpu.make_async_remote_copy(
            src_ref=partial.at[peer], dst_ref=partials.at[peer],
            send_sem=c_send.at[peer], recv_sem=c_recv.at[peer], device_id=(f, peer), device_id_type=MESH)

    with jax.named_scope("forward"):
        for r in range(FROWS):
            for comp in range(2):
                total = parts[r, comp].astype(jnp.float32)
                for g in range(r + FROWS, nf, FROWS):
                    total = total + parts[g, comp].astype(jnp.float32)
                result[r, comp] = total

        def forward_step(s, _):
            cos_phi = phase[0, s]
            sin_phi = phase[1, s]
            for r in range(FROWS):
                a = result[r, 0]
                b = result[r, 1]
                lhs[r * cols:(r + 1) * cols, :rows] = (a * cos_phi + b * sin_phi).astype(jnp.bfloat16)
                lhs[r * cols:(r + 1) * cols, rows:] = (b * cos_phi - a * sin_phi).astype(jnp.bfloat16)
            acc[...] = jnp.dot(lhs[...], table[...], preferred_element_type=jnp.float32)
            total_re = jnp.zeros((cols, half), jnp.float32)
            total_im = jnp.zeros((cols, half), jnp.float32)
            for r in range(FROWS):
                cos_psi, sin_psi = psi(r, s)
                re = acc[r * cols:(r + 1) * cols, :half]
                im = acc[r * cols:(r + 1) * cols, half:]
                total_re = total_re + re * cos_psi + im * sin_psi
                total_im = total_im + im * cos_psi - re * sin_psi
            total_re = (total_re * scale).astype(jnp.bfloat16)
            total_im = (total_im * scale).astype(jnp.bfloat16)
            for q in range(chunks):
                peer = s * chunks + q
                partial[peer, 0] = total_re[:, q * chunk:(q + 1) * chunk]
                partial[peer, 1] = total_im[:, q * chunk:(q + 1) * chunk]

                @pl.when(peer != t)
                def _():
                    send_partial(peer).start()
            return 0

        lax.fori_loop(0, NSUB, forward_step, 0)

    with jax.named_scope("weigh"):
        @pl.when(apart)
        def _():
            send_vis.wait_recv()
            send_factor.wait_recv()

        def add_partial(i, total):
            peer = strip_peer(i)
            arrive_partial(peer).wait_recv()
            return total + partials[peer].astype(jnp.float32)

        model = lax.fori_loop(1, ns, add_partial, partial[t].astype(jnp.float32))
        resid[t] = (factor_here[...][None] * (vis_here[...] - model)).astype(jnp.bfloat16)

    def send_resid(peer):
        return pltpu.make_async_remote_copy(
            src_ref=resid.at[t], dst_ref=resid.at[t],
            send_sem=e_send.at[peer], recv_sem=e_recv.at[t], device_id=(f, peer), device_id_type=MESH)

    def arrive_resid(peer):
        return pltpu.make_async_remote_copy(
            src_ref=resid.at[peer], dst_ref=resid.at[peer],
            send_sem=e_send.at[peer], recv_sem=e_recv.at[peer], device_id=(f, peer), device_id_type=MESH)

    def start_resid(i, _):
        send_resid(strip_peer(i)).start()
        return 0

    def wait_resid(i, _):
        arrive_resid(strip_peer(i)).wait_recv()
        return 0

    lax.fori_loop(1, ns, start_resid, 0)
    lax.fori_loop(1, ns, wait_resid, 0)

    def send_update(r, peer):
        return pltpu.make_async_remote_copy(
            src_ref=lhs_out(r), dst_ref=out.at[0, :, facet_columns(f), :],
            send_sem=g_send.at[peer], recv_sem=g_recv.at[f], device_id=(peer, t), device_id_type=MESH)

    def lhs_out(r):
        return parts.at[r]

    def own_update(r):
        return pltpu.make_async_copy(lhs_out(r), out.at[0, :, facet_columns(f), :], local_sem.at[1])

    def arrive_update(peer):
        return pltpu.make_async_remote_copy(
            src_ref=parts.at[0], dst_ref=out.at[0, :, facet_columns(peer), :],
            send_sem=g_send.at[peer], recv_sem=g_recv.at[peer], device_id=(peer, t), device_id_type=MESH)

    with jax.named_scope("adjoint"):
        def adjoint_step(r, _):
            for s in range(NSUB):
                cos_psi, sin_psi = psi(r, s)
                for q in range(chunks):
                    g = resid[s * chunks + q, 0].astype(jnp.float32)
                    h = resid[s * chunks + q, 1].astype(jnp.float32)
                    c = cos_psi[:, q * chunk:(q + 1) * chunk]
                    d = sin_psi[:, q * chunk:(q + 1) * chunk]
                    lhs[s * cols:(s + 1) * cols, q * chunk:(q + 1) * chunk] = (g * c - h * d).astype(jnp.bfloat16)
                    lhs[s * cols:(s + 1) * cols, half + q * chunk:half + (q + 1) * chunk] = (h * c + g * d).astype(jnp.bfloat16)
            acc[...] = lax.dot_general(
                lhs[...], table[...], (((1,), (1,)), ((), ())), preferred_element_type=jnp.float32)
            total_re = jnp.zeros((cols, rows), jnp.float32)
            total_im = jnp.zeros((cols, rows), jnp.float32)
            for s in range(NSUB):
                cos_phi = phase[0, s]
                sin_phi = phase[1, s]
                p = acc[s * cols:(s + 1) * cols, :rows]
                q = acc[s * cols:(s + 1) * cols, rows:]
                total_re = total_re + p * cos_phi - q * sin_phi
                total_im = total_im + q * cos_phi + p * sin_phi
            parts[r, 0] = (total_re * scale).astype(jnp.bfloat16)
            parts[r, 1] = (total_im * scale).astype(jnp.bfloat16)

            def start_update(i, _):
                peer = i * FROWS + r

                @pl.when(peer != f)
                def _():
                    send_update(r, peer).start()

                @pl.when(peer == f)
                def _():
                    own_update(r).start()
                return 0

            lax.fori_loop(0, nf // FROWS, start_update, 0)
            return 0

        lax.fori_loop(0, FROWS, adjoint_step, 0)

    with jax.named_scope("drain"):
        def drain_strip(i, _):
            peer = strip_peer(i)
            send_partial(peer).wait_send()
            send_resid(peer).wait_send()
            return 0

        def drain_facet(i, _):
            peer = facet_peer(i)
            send_part(peer).wait_send()
            send_update(0, peer).wait_send()
            arrive_update(peer).wait_recv()
            return 0

        lax.fori_loop(1, ns, drain_strip, 0)
        lax.fori_loop(1, nf, drain_facet, 0)
        own_update(0).wait()

        @pl.when(apart)
        def _():
            send_vis.wait_send()
            send_factor.wait_send()


def on_device(nf, ns, facets, offsets, visibilities, weights, mask):
    _, _, columns, rows = facets.shape
    cols = columns // nf
    frequencies = visibilities.shape[2] * nf
    half = frequencies // NSUB
    chunk = frequencies // ns
    vmem = pl.BlockSpec(memory_space=pltpu.VMEM)
    anywhere = pl.BlockSpec(memory_space=pl.ANY)
    dma = pltpu.SemaphoreType.DMA
    flops = 2 * 2 * FROWS * NSUB * cols * (2 * rows) * (2 * half)
    return pl.pallas_call(
        functools.partial(kernel, nf, ns),
        out_shape=jax.ShapeDtypeStruct(facets.shape, jnp.bfloat16),
        in_specs=[anywhere, pl.BlockSpec(memory_space=pltpu.SMEM), vmem, vmem, vmem],
        out_specs=anywhere,
        scratch_shapes=[
            pltpu.VMEM((nf, 2, cols, rows), jnp.bfloat16),
            pltpu.VMEM((2 * rows, 2 * half), jnp.bfloat16),
            pltpu.VMEM((2, NSUB, 1, rows), jnp.float32),
            pltpu.VMEM((NSUB * cols, 2 * max(half, rows)), jnp.bfloat16),
            pltpu.VMEM((NSUB * cols, 2 * max(half, rows)), jnp.float32),
            pltpu.VMEM(weights.shape, jnp.float32),
            pltpu.VMEM(visibilities.shape, jnp.float32),
            pltpu.VMEM(weights.shape, jnp.float32),
            pltpu.VMEM((ns, 2, cols, chunk), jnp.bfloat16),
            pltpu.VMEM((ns, 2, cols, chunk), jnp.bfloat16),
            pltpu.VMEM((ns, 2, cols, chunk), jnp.bfloat16),
            pltpu.VMEM((FROWS, 2, cols, rows), jnp.float32),
            dma((nf,)), dma((nf,)), dma((2,)), dma((2,)), dma((ns,)), dma((ns,)), dma((ns,)), dma((ns,)),
            dma((nf,)), dma((nf,)), dma((2,)),
        ],
        cost_estimate=pl.CostEstimate(flops=flops, bytes_accessed=4 * facets.size, transcendentals=0),
        compiler_params=pltpu.CompilerParams(
            collective_id=0, has_side_effects=True, vmem_limit_bytes=48 * 1024 * 1024),
    )(facets, offsets, visibilities, weights, mask)


def solution(mesh):
    placed = (
        P("facet", None, None, "strip"),
        P(),
        P(None, "strip", "facet"),
        P("strip", "facet"),
        P("strip", "facet"),
    )
    return jax.shard_map(
        functools.partial(on_device, mesh.shape["facet"], mesh.shape["strip"]),
        mesh=mesh,
        in_specs=placed,
        out_specs=P("facet", None, None, "strip"),
        check_vma=False,
    )
```

```python
import functools
import math

import jax
import jax.numpy as jnp
from jax import lax
from jax.experimental import pallas as pl
from jax.experimental.pallas import tpu as pltpu
from jax.sharding import PartitionSpec as P

NSUB = 4
FROWS = 4
MESH = pl.DeviceIdType.MESH


def turn(count, cells):
    quarter = cells // 4
    shift = quarter.bit_length() - 1
    quadrant = (count + quarter // 2) >> shift
    angle = (count - (quadrant << shift)).astype(jnp.float32) * (2.0 * math.pi / cells)
    square = angle * angle
    sine = angle * (1.0 + square * (-1.0 / 6 + square * (1.0 / 120 + square * (-1.0 / 5040 + square * (1.0 / 362880)))))
    cosine = 1.0 + square * (-0.5 + square * (1.0 / 24 + square * (-1.0 / 720 + square * (1.0 / 40320))))
    odd = (quadrant & 1) == 1
    first = jnp.where(odd, sine, cosine)
    second = jnp.where(odd, cosine, sine)
    cos_value = jnp.where(((quadrant + 1) & 2) == 2, -first, first)
    sin_value = jnp.where((quadrant & 2) == 2, -second, second)
    return cos_value, sin_value


def quarter_turn(count):
    part = count & 3
    sign = jnp.where(part >= 2, -1.0, 1.0)
    even = (part & 1) == 0
    return jnp.where(even, sign, 0.0), jnp.where(even, 0.0, sign)


PASSES = 2


def kernel(
    nf, ns,
    facets, offsets_in, vis, weights_in, mask_in, out,
    offsets, weights, mask, mine, relayed, joint, parts, table, phase, lhs, acc, factor, vis_here, factor_here, partial, partials, resid, sums, update,
    r_send, r_recv, a_send, a_recv, v_send, v_recv, c_send, c_recv, e_send, e_recv, g_send, f_send, g_recv, g_local, local_sem,
):
    f = lax.axis_index("facet")
    t = lax.axis_index("strip")
    cols, rows = parts.shape[4], parts.shape[5]
    cells = FROWS * rows * ns
    half = table.shape[1] // 2
    chunk = partial.shape[4]
    chunks = half // chunk
    scale = 1.0 / math.sqrt(rows * ns)
    start = t * rows
    apart = f != t

    depth = nf // 2
    z = lax.div(f, 2)
    x = lax.rem(f, 2)
    odd = lax.rem(z, 2)

    def facet_at(dz, side):
        return lax.rem(z + dz + depth, depth) * 2 + side

    def strip_peer(i):
        return lax.rem(t + i, ns)

    def columns_of(g, p):
        return pl.ds(pl.multiple_of((g * PASSES + p) * cols, cols), cols)

    barrier = pltpu.get_barrier_semaphore()

    def greet_strip(i, _):
        pl.semaphore_signal(barrier, inc=1, device_id=(f, strip_peer(i)), device_id_type=MESH)
        return 0

    for dz in (1, -1, 2, -2):
        for side in range(2):
            pl.semaphore_signal(barrier, inc=1, device_id=(facet_at(dz, side), t), device_id_type=MESH)
    pl.semaphore_signal(barrier, inc=1, device_id=(facet_at(0, 1 - x), t), device_id_type=MESH)
    lax.fori_loop(1, ns, greet_strip, 0)

    @pl.when(apart)
    def _():
        pl.semaphore_signal(barrier, inc=1, device_id=(t, f), device_id_type=MESH)

    get_offsets = pltpu.make_async_copy(offsets_in, offsets, local_sem.at[0])
    get_weights = pltpu.make_async_copy(weights_in, weights, local_sem.at[1])
    get_mask = pltpu.make_async_copy(mask_in, mask, local_sem.at[2])
    get_vis = pltpu.make_async_copy(vis, vis_here, local_sem.at[3])
    get_offsets.start()
    get_weights.start()
    get_mask.start()
    get_mine = pltpu.make_async_copy(facets.at[0], mine, local_sem.at[4])
    get_mine.start()

    pl.semaphore_wait(barrier, 9 + ns - 1 + apart.astype(jnp.int32))

    routes = (((1, 0), (1, 1), (2, 0)), ((-1, 0), (-1, 1), (-2, 1)))
    place = {1: 0, -1: 1, 2: 2, -2: 3, 0: 4}

    def relay(p, way, u):
        step = 2 - 4 * way
        dz, side = routes[way][u]
        return pltpu.make_async_remote_copy(
            src_ref=facets.at[0, :, columns_of(facet_at(dz + step, side), p), :], dst_ref=relayed.at[p, way, u],
            send_sem=r_send.at[p, way, u], recv_sem=r_recv.at[p, way, u],
            device_id=(facet_at(step, x), t), device_id_type=MESH)

    def joined(p, way, u):
        dz, side = routes[way][u]
        return pltpu.make_async_remote_copy(
            src_ref=joint.at[p, way, u], dst_ref=parts.at[p, place[dz], x],
            send_sem=a_send.at[p, 3 * way + u], recv_sem=a_recv.at[p, place[dz], x],
            device_id=(facet_at(dz, side), t), device_id_type=MESH)

    def direct(p, n):
        dz, side = ((2, 1), (-2, 0), (0, 1 - x))[n]
        peer = facet_at(dz, side)
        return pltpu.make_async_remote_copy(
            src_ref=facets.at[0, :, columns_of(peer, p), :], dst_ref=parts.at[p, place[dz], x],
            send_sem=a_send.at[p, 6 + n], recv_sem=a_recv.at[p, place[dz], x],
            device_id=(peer, t), device_id_type=MESH)

    def arrive_part(p, k, side):
        return pltpu.make_async_remote_copy(
            src_ref=parts.at[p, k, side], dst_ref=parts.at[p, k, side],
            send_sem=a_send.at[p, 0], recv_sem=a_recv.at[p, k, side],
            device_id=(facet_at(0, 1 - x), t), device_id_type=MESH)

    def start_relays(p):
        for u in range(3):
            for way in range(2):
                relay(p, way, u).start()
        for n in range(3):
            direct(p, n).start()

    def join(p):
        for u in range(3):
            for way in range(2):
                relay(p, way, u).wait_recv()
                own = mine[:, columns_of(facet_at(*routes[way][u]), p), :]
                joint[p, way, u] = (relayed[p, way, u].astype(jnp.float32) + own.astype(jnp.float32)).astype(jnp.bfloat16)
                joined(p, way, u).start()

    start_relays(0)
    get_weights.wait()
    get_mask.wait()
    factor[...] = weights[...] * mask[...].astype(jnp.float32)
    send_vis = pltpu.make_async_remote_copy(
        src_ref=vis, dst_ref=vis_here, send_sem=v_send.at[0], recv_sem=v_recv.at[0], device_id=(t, f), device_id_type=MESH)
    send_factor = pltpu.make_async_remote_copy(
        src_ref=factor, dst_ref=factor_here, send_sem=v_send.at[1], recv_sem=v_recv.at[1], device_id=(t, f), device_id_type=MESH)

    @pl.when(apart)
    def _():
        send_vis.start()
        send_factor.start()

    @pl.when(jnp.logical_not(apart))
    def _():
        get_vis.start()
        factor_here[...] = factor[...]
        get_vis.wait()

    get_offsets.wait()

    with jax.named_scope("tables"):
        block = min(32, rows)

        def fill(i, _):
            base = pl.multiple_of(i * block, block)
            row = start + base + lax.broadcasted_iota(jnp.int32, (block, half), 0)
            j = lax.broadcasted_iota(jnp.int32, (block, half), 1)
            cos_value, sin_value = turn((row * j) & (cells - 1), cells)
            low = pl.ds(base, block)
            high = pl.ds(pl.multiple_of(rows + base, block), block)
            cos_value = cos_value.astype(jnp.bfloat16)
            table[low, :half] = cos_value
            table[high, half:] = cos_value
            table[low, half:] = (-sin_value).astype(jnp.bfloat16)
            table[high, :half] = sin_value.astype(jnp.bfloat16)
            return 0

        lax.fori_loop(0, rows // block, fill, 0)
        for s in range(NSUB):
            row = start + lax.broadcasted_iota(jnp.int32, (1, rows), 1)
            cos_value, sin_value = turn((row * offsets[s]) & (cells - 1), cells)
            phase[0, s] = cos_value
            phase[1, s] = sin_value

    get_mine.wait()
    for p in range(PASSES):
        join(p)
        if p + 1 < PASSES:
            start_relays(p + 1)

    def psi(r, s):
        j = lax.broadcasted_iota(jnp.int32, (1, half), 1)
        return quarter_turn((offsets[s] + j) * (r + 2))

    def send_partial(peer, p):
        return pltpu.make_async_remote_copy(
            src_ref=partial.at[p, peer], dst_ref=partials.at[p, t],
            send_sem=c_send.at[p, peer], recv_sem=c_recv.at[p, t], device_id=(f, peer), device_id_type=MESH)

    def arrive_partial(peer, p):
        return pltpu.make_async_remote_copy(
            src_ref=partial.at[p, peer], dst_ref=partials.at[p, peer],
            send_sem=c_send.at[p, peer], recv_sem=c_recv.at[p, peer], device_id=(f, peer), device_id_type=MESH)

    def send_resid(peer, p):
        return pltpu.make_async_remote_copy(
            src_ref=resid.at[p, t], dst_ref=resid.at[p, t],
            send_sem=e_send.at[p, peer], recv_sem=e_recv.at[p, t], device_id=(f, peer), device_id_type=MESH)

    def arrive_resid(peer, p):
        return pltpu.make_async_remote_copy(
            src_ref=resid.at[p, peer], dst_ref=resid.at[p, peer],
            send_sem=e_send.at[p, peer], recv_sem=e_recv.at[p, peer], device_id=(f, peer), device_id_type=MESH)

    spread = ((1, 0), (1, 1), (-1, 0), (-1, 1), (2, 0), (2, 1), (-2, 0), (-2, 1), (0, 1 - x))
    passed = ((-1, 0, 2), (1, 0, -2), (-1, 1, 2), (1, 1, -2), (-2, 0, 2), (2, 1, -2))

    def residue_at(dz, side):
        return lax.rem(odd + dz + 2, 2) * 2 + side

    def send_update(p, n):
        dz, side = spread[n]
        return pltpu.make_async_remote_copy(
            src_ref=update.at[p, residue_at(dz, side)], dst_ref=out.at[0, :, columns_of(f, p), :],
            send_sem=g_send.at[p, n], recv_sem=g_recv.at[p, f],
            device_id=(facet_at(dz, side), t), device_id_type=MESH)

    def pass_on(p, n):
        dz, side, step = passed[n]
        block = out.at[0, :, columns_of(facet_at(dz, side), p), :]
        return pltpu.make_async_remote_copy(
            src_ref=block, dst_ref=block,
            send_sem=f_send.at[p, n], recv_sem=g_recv.at[p, facet_at(dz, side)],
            device_id=(facet_at(step, x), t), device_id_type=MESH)

    def own_update(p):
        return pltpu.make_async_copy(update.at[p, residue_at(0, x)], out.at[0, :, columns_of(f, p), :], g_local.at[p])

    def arrive_update(p, peer):
        return pltpu.make_async_remote_copy(
            src_ref=update.at[p, 0], dst_ref=out.at[0, :, columns_of(peer, p), :],
            send_sem=g_send.at[p, 0], recv_sem=g_recv.at[p, peer],
            device_id=(facet_at(0, 1 - x), t), device_id_type=MESH)

    def relay_updates(p):
        for n in range(6):
            dz, side, _ = passed[n]
            arrive_update(p, facet_at(dz, side)).wait_recv()
            pass_on(p, n).start()

    def forward(p):
        for k in range(4):
            for side in range(2):
                arrive_part(p, k, side).wait_recv()
        arrive_part(p, 4, 1 - x).wait_recv()
        parts[p, 4, x] = mine[:, columns_of(f, p), :]
        for side in range(2):
            same = residue_at(0, side)
            other = residue_at(1, side)
            two = parts[p, 2, side].astype(jnp.float32) + parts[p, 3, side].astype(jnp.float32)
            sums[same] = two + parts[p, 4, side].astype(jnp.float32)
            sums[other] = parts[p, 0, side].astype(jnp.float32) + parts[p, 1, side].astype(jnp.float32)
        for s in range(NSUB):
            cos_phi = phase[0, s]
            sin_phi = phase[1, s]
            for r in range(FROWS):
                a = sums[r, 0]
                b = sums[r, 1]
                row = (s * FROWS + r) * cols
                lhs[row:row + cols, :rows] = (a * cos_phi + b * sin_phi).astype(jnp.bfloat16)
                lhs[row:row + cols, rows:] = (b * cos_phi - a * sin_phi).astype(jnp.bfloat16)
        acc[...] = jnp.dot(lhs[...], table[...], preferred_element_type=jnp.float32)
        for s in range(NSUB):
            total_re = jnp.zeros((cols, half), jnp.float32)
            total_im = jnp.zeros((cols, half), jnp.float32)
            for r in range(FROWS):
                cos_psi, sin_psi = psi(r, s)
                row = (s * FROWS + r) * cols
                re = acc[row:row + cols, :half]
                im = acc[row:row + cols, half:]
                total_re = total_re + re * cos_psi + im * sin_psi
                total_im = total_im + im * cos_psi - re * sin_psi
            total_re = (total_re * scale).astype(jnp.bfloat16)
            total_im = (total_im * scale).astype(jnp.bfloat16)
            for q in range(chunks):
                peer = s * chunks + q
                partial[p, peer, 0] = total_re[:, q * chunk:(q + 1) * chunk]
                partial[p, peer, 1] = total_im[:, q * chunk:(q + 1) * chunk]

        def start_partial(i, _):
            send_partial(strip_peer(i), p).start()
            return 0

        lax.fori_loop(1, ns, start_partial, 0)

    def weigh(p):
        if p == 0:
            @pl.when(apart)
            def _():
                send_vis.wait_recv()
                send_factor.wait_recv()

        def add_partial(i, total):
            peer = strip_peer(i)
            arrive_partial(peer, p).wait_recv()
            return total + partials[p, peer].astype(jnp.float32)

        model = lax.fori_loop(1, ns, add_partial, partial[p, t].astype(jnp.float32))
        mine = slice(p * cols, (p + 1) * cols)
        resid[p, t] = (factor_here[mine][None] * (vis_here[:, mine] - model)).astype(jnp.bfloat16)

        def start_resid(i, _):
            send_resid(strip_peer(i), p).start()
            return 0

        lax.fori_loop(1, ns, start_resid, 0)

    def adjoint(p):
        def wait_resid(i, _):
            arrive_resid(strip_peer(i), p).wait_recv()
            return 0

        lax.fori_loop(1, ns, wait_resid, 0)
        for r in range(FROWS):
            for s in range(NSUB):
                cos_psi, sin_psi = psi(r, s)
                row = (r * NSUB + s) * cols
                for q in range(chunks):
                    g = resid[p, s * chunks + q, 0].astype(jnp.float32)
                    h = resid[p, s * chunks + q, 1].astype(jnp.float32)
                    c = cos_psi[:, q * chunk:(q + 1) * chunk]
                    d = sin_psi[:, q * chunk:(q + 1) * chunk]
                    lhs[row:row + cols, q * chunk:(q + 1) * chunk] = (g * c - h * d).astype(jnp.bfloat16)
                    lhs[row:row + cols, half + q * chunk:half + (q + 1) * chunk] = (h * c + g * d).astype(jnp.bfloat16)
        acc[...] = lax.dot_general(
            lhs[...], table[...], (((1,), (1,)), ((), ())), preferred_element_type=jnp.float32)
        for r in range(FROWS):
            total_re = jnp.zeros((cols, rows), jnp.float32)
            total_im = jnp.zeros((cols, rows), jnp.float32)
            for s in range(NSUB):
                cos_phi = phase[0, s]
                sin_phi = phase[1, s]
                row = (r * NSUB + s) * cols
                a = acc[row:row + cols, :rows]
                b = acc[row:row + cols, rows:]
                total_re = total_re + a * cos_phi - b * sin_phi
                total_im = total_im + b * cos_phi + a * sin_phi
            update[p, r, 0] = (total_re * scale).astype(jnp.bfloat16)
            update[p, r, 1] = (total_im * scale).astype(jnp.bfloat16)

        own_update(p).start()
        for n in range(9):
            send_update(p, n).start()

    with jax.named_scope("transforms"):
        forward(0)
        weigh(0)
        forward(1)
        adjoint(0)
        weigh(1)
        relay_updates(0)
        adjoint(1)
        relay_updates(1)

    with jax.named_scope("drain"):
        for p in range(PASSES):
            def drain_strip(i, _):
                peer = strip_peer(i)
                send_partial(peer, p).wait_send()
                send_resid(peer, p).wait_send()
                return 0

            lax.fori_loop(1, ns, drain_strip, 0)
            for u in range(3):
                for way in range(2):
                    relay(p, way, u).wait_send()
                    joined(p, way, u).wait_send()
                direct(p, u).wait_send()
            for n in range(9):
                send_update(p, n).wait_send()
            for n in range(6):
                pass_on(p, n).wait_send()
            own_update(p).wait()
            arrive_update(p, facet_at(0, 1 - x)).wait_recv()
            for dz, side in ((-2, 1), (2, 0), (3, 0), (3, 1), (-3, 0), (-3, 1), (4, 0), (4, 1)):
                arrive_update(p, facet_at(dz, side)).wait_recv()

        @pl.when(apart)
        def _():
            send_vis.wait_send()
            send_factor.wait_send()


def on_device(nf, ns, facets, offsets, visibilities, weights, mask):
    _, _, columns, rows = facets.shape
    cols = columns // nf // PASSES
    frequencies = visibilities.shape[2] * nf
    half = frequencies // NSUB
    chunk = frequencies // ns
    hbm = pl.BlockSpec(memory_space=pltpu.HBM)
    dma = pltpu.SemaphoreType.DMA
    flops = 2 * 2 * FROWS * NSUB * cols * PASSES * (2 * rows) * (2 * half)
    exchanged = (PASSES, ns, 2, cols, chunk)
    return pl.pallas_call(
        functools.partial(kernel, nf, ns),
        out_shape=jax.ShapeDtypeStruct(facets.shape, jnp.bfloat16),
        in_specs=[hbm] * 5,
        out_specs=hbm,
        scratch_shapes=[
            pltpu.SMEM(offsets.shape, jnp.int32),
            pltpu.VMEM(weights.shape, jnp.float32),
            pltpu.VMEM(mask.shape, jnp.int32),
            pltpu.VMEM((2, columns, rows), jnp.bfloat16),
            pltpu.VMEM((PASSES, 2, 3, 2, cols, rows), jnp.bfloat16),
            pltpu.VMEM((PASSES, 2, 3, 2, cols, rows), jnp.bfloat16),
            pltpu.VMEM((PASSES, 5, 2, 2, cols, rows), jnp.bfloat16),
            pltpu.VMEM((2 * rows, 2 * half), jnp.bfloat16),
            pltpu.VMEM((2, NSUB, 1, rows), jnp.float32),
            pltpu.VMEM((FROWS * NSUB * cols, 2 * max(half, rows)), jnp.bfloat16),
            pltpu.VMEM((FROWS * NSUB * cols, 2 * max(half, rows)), jnp.float32),
            pltpu.VMEM(weights.shape, jnp.float32),
            pltpu.VMEM(visibilities.shape, jnp.float32),
            pltpu.VMEM(weights.shape, jnp.float32),
            pltpu.VMEM(exchanged, jnp.bfloat16),
            pltpu.VMEM(exchanged, jnp.bfloat16),
            pltpu.VMEM(exchanged, jnp.bfloat16),
            pltpu.VMEM((FROWS, 2, cols, rows), jnp.float32),
            pltpu.VMEM((PASSES, FROWS, 2, cols, rows), jnp.bfloat16),
            dma((PASSES, 2, 3)), dma((PASSES, 2, 3)), dma((PASSES, 9)), dma((PASSES, 5, 2)), dma((2,)), dma((2,)),
            dma((PASSES, ns)), dma((PASSES, ns)), dma((PASSES, ns)), dma((PASSES, ns)),
            dma((PASSES, 9)), dma((PASSES, 6)), dma((PASSES, nf)), dma((PASSES,)), dma((5,)),
        ],
        cost_estimate=pl.CostEstimate(flops=flops, bytes_accessed=4 * facets.size, transcendentals=0),
        compiler_params=pltpu.CompilerParams(
            collective_id=0, has_side_effects=True, vmem_limit_bytes=62 * 1024 * 1024),
    )(facets, offsets, visibilities, weights, mask)


def solution(mesh):
    placed = (
        P("facet", None, None, "strip"),
        P(),
        P(None, "strip", "facet"),
        P("strip", "facet"),
        P("strip", "facet"),
    )
    return jax.shard_map(
        functools.partial(on_device, mesh.shape["facet"], mesh.shape["strip"]),
        mesh=mesh,
        in_specs=placed,
        out_specs=P("facet", None, None, "strip"),
        check_vma=False,
    )
```

```python
import functools
import math

import jax
import jax.numpy as jnp
from jax import lax
from jax.experimental import pallas as pl
from jax.experimental.pallas import tpu as pltpu
from jax.sharding import PartitionSpec as P

NSUB = 4
FROWS = 4
MESH = pl.DeviceIdType.MESH


def turn(count, cells):
    quarter = cells // 4
    shift = quarter.bit_length() - 1
    quadrant = (count + quarter // 2) >> shift
    angle = (count - (quadrant << shift)).astype(jnp.float32) * (2.0 * math.pi / cells)
    square = angle * angle
    sine = angle * (1.0 + square * (-1.0 / 6 + square * (1.0 / 120 + square * (-1.0 / 5040 + square * (1.0 / 362880)))))
    cosine = 1.0 + square * (-0.5 + square * (1.0 / 24 + square * (-1.0 / 720 + square * (1.0 / 40320))))
    odd = (quadrant & 1) == 1
    first = jnp.where(odd, sine, cosine)
    second = jnp.where(odd, cosine, sine)
    cos_value = jnp.where(((quadrant + 1) & 2) == 2, -first, first)
    sin_value = jnp.where((quadrant & 2) == 2, -second, second)
    return cos_value, sin_value


def quarter_turn(count):
    part = count & 3
    sign = jnp.where(part >= 2, -1.0, 1.0)
    even = (part & 1) == 0
    return jnp.where(even, sign, 0.0), jnp.where(even, 0.0, sign)


PASSES = 2


def kernel(
    nf, ns,
    facets, offsets_in, vis, weights_in, mask_in, out,
    offsets, weights, mask, mine, relayed, joint, parts, table, phase, lhs, acc, factor, vis_here, factor_here, partial, partials, resid, sums, update,
    r_send, r_recv, a_send, a_recv, v_send, v_recv, c_send, c_recv, e_send, e_recv, g_send, f_send, g_recv, g_local, local_sem,
):
    f = lax.axis_index("facet")
    t = lax.axis_index("strip")
    cols, rows = parts.shape[4], parts.shape[5]
    cells = FROWS * rows * ns
    half = table.shape[1] // 2
    chunk = partial.shape[4]
    chunks = half // chunk
    scale = 1.0 / math.sqrt(rows * ns)
    start = t * rows
    apart = f != t

    depth = nf // 2
    z = lax.div(f, 2)
    x = lax.rem(f, 2)
    odd = lax.rem(z, 2)

    def facet_at(dz, side):
        return lax.rem(z + dz + depth, depth) * 2 + side

    def strip_peer(i):
        return lax.rem(t + i, ns)

    def columns_of(g, p):
        return pl.ds(pl.multiple_of((g * PASSES + p) * cols, cols), cols)

    barrier = pltpu.get_barrier_semaphore()

    def greet_strip(i, _):
        pl.semaphore_signal(barrier, inc=1, device_id=(f, strip_peer(i)), device_id_type=MESH)
        return 0

    for dz in (1, -1, 2, -2):
        for side in range(2):
            pl.semaphore_signal(barrier, inc=1, device_id=(facet_at(dz, side), t), device_id_type=MESH)
    pl.semaphore_signal(barrier, inc=1, device_id=(facet_at(0, 1 - x), t), device_id_type=MESH)
    lax.fori_loop(1, ns, greet_strip, 0)

    @pl.when(apart)
    def _():
        pl.semaphore_signal(barrier, inc=1, device_id=(t, f), device_id_type=MESH)

    get_offsets = pltpu.make_async_copy(offsets_in, offsets, local_sem.at[0])
    get_weights = pltpu.make_async_copy(weights_in, weights, local_sem.at[1])
    get_mask = pltpu.make_async_copy(mask_in, mask, local_sem.at[2])
    get_vis = pltpu.make_async_copy(vis, vis_here, local_sem.at[3])
    get_offsets.start()
    get_weights.start()
    get_mask.start()
    get_mine = pltpu.make_async_copy(facets.at[0], mine, local_sem.at[4])
    get_mine.start()

    pl.semaphore_wait(barrier, 9 + ns - 1 + apart.astype(jnp.int32))

    routes = (((1, 0), (1, 1), (2, 0)), ((-1, 0), (-1, 1), (-2, 1)))
    place = {1: 0, -1: 1, 2: 2, -2: 3, 0: 4}

    def relay(p, way, u):
        step = 2 - 4 * way
        dz, side = routes[way][u]
        return pltpu.make_async_remote_copy(
            src_ref=facets.at[0, :, columns_of(facet_at(dz + step, side), p), :], dst_ref=relayed.at[p, way, u],
            send_sem=r_send.at[p, way, u], recv_sem=r_recv.at[p, way, u],
            device_id=(facet_at(step, x), t), device_id_type=MESH)

    def joined(p, way, u):
        dz, side = routes[way][u]
        return pltpu.make_async_remote_copy(
            src_ref=joint.at[p, way, u], dst_ref=parts.at[p, place[dz], x],
            send_sem=a_send.at[p, 3 * way + u], recv_sem=a_recv.at[p, place[dz], x],
            device_id=(facet_at(dz, side), t), device_id_type=MESH)

    def direct(p, n):
        dz, side = ((2, 1), (-2, 0), (0, 1 - x))[n]
        peer = facet_at(dz, side)
        return pltpu.make_async_remote_copy(
            src_ref=facets.at[0, :, columns_of(peer, p), :], dst_ref=parts.at[p, place[dz], x],
            send_sem=a_send.at[p, 6 + n], recv_sem=a_recv.at[p, place[dz], x],
            device_id=(peer, t), device_id_type=MESH)

    def arrive_part(p, k, side):
        return pltpu.make_async_remote_copy(
            src_ref=parts.at[p, k, side], dst_ref=parts.at[p, k, side],
            send_sem=a_send.at[p, 0], recv_sem=a_recv.at[p, k, side],
            device_id=(facet_at(0, 1 - x), t), device_id_type=MESH)

    def start_relays(p):
        for u in range(3):
            for way in range(2):
                relay(p, way, u).start()
        for n in range(3):
            direct(p, n).start()

    def join(p):
        for u in range(3):
            for way in range(2):
                relay(p, way, u).wait_recv()
                own = mine[:, columns_of(facet_at(*routes[way][u]), p), :]
                joint[p, way, u] = (relayed[p, way, u].astype(jnp.float32) + own.astype(jnp.float32)).astype(jnp.bfloat16)
                joined(p, way, u).start()
                if p + 1 < PASSES:
                    relay(p + 1, way, u).start()
        if p + 1 < PASSES:
            for n in range(3):
                direct(p + 1, n).start()

    start_relays(0)
    get_weights.wait()
    get_mask.wait()
    factor[...] = weights[...] * mask[...].astype(jnp.float32)
    send_vis = pltpu.make_async_remote_copy(
        src_ref=vis, dst_ref=vis_here, send_sem=v_send.at[0], recv_sem=v_recv.at[0], device_id=(t, f), device_id_type=MESH)
    send_factor = pltpu.make_async_remote_copy(
        src_ref=factor, dst_ref=factor_here, send_sem=v_send.at[1], recv_sem=v_recv.at[1], device_id=(t, f), device_id_type=MESH)

    @pl.when(apart)
    def _():
        send_vis.start()
        send_factor.start()

    @pl.when(jnp.logical_not(apart))
    def _():
        get_vis.start()
        factor_here[...] = factor[...]
        get_vis.wait()

    get_offsets.wait()

    with jax.named_scope("tables"):
        block = min(32, rows)

        def fill(i, _):
            base = pl.multiple_of(i * block, block)
            row = start + base + lax.broadcasted_iota(jnp.int32, (block, half), 0)
            j = lax.broadcasted_iota(jnp.int32, (block, half), 1)
            cos_value, sin_value = turn((row * j) & (cells - 1), cells)
            low = pl.ds(base, block)
            high = pl.ds(pl.multiple_of(rows + base, block), block)
            cos_value = cos_value.astype(jnp.bfloat16)
            table[low, :half] = cos_value
            table[high, half:] = cos_value
            table[low, half:] = (-sin_value).astype(jnp.bfloat16)
            table[high, :half] = sin_value.astype(jnp.bfloat16)
            return 0

        lax.fori_loop(0, rows // block, fill, 0)
        for s in range(NSUB):
            row = start + lax.broadcasted_iota(jnp.int32, (1, rows), 1)
            cos_value, sin_value = turn((row * offsets[s]) & (cells - 1), cells)
            phase[0, s] = cos_value
            phase[1, s] = sin_value

    get_mine.wait()
    for p in range(PASSES):
        join(p)

    def psi(r, s):
        j = lax.broadcasted_iota(jnp.int32, (1, half), 1)
        return quarter_turn((offsets[s] + j) * (r + 2))

    def send_partial(peer, p):
        return pltpu.make_async_remote_copy(
            src_ref=partial.at[p, peer], dst_ref=partials.at[p, t],
            send_sem=c_send.at[p, peer], recv_sem=c_recv.at[p, t], device_id=(f, peer), device_id_type=MESH)

    def arrive_partial(peer, p):
        return pltpu.make_async_remote_copy(
            src_ref=partial.at[p, peer], dst_ref=partials.at[p, peer],
            send_sem=c_send.at[p, peer], recv_sem=c_recv.at[p, peer], device_id=(f, peer), device_id_type=MESH)

    def send_resid(peer, p):
        return pltpu.make_async_remote_copy(
            src_ref=resid.at[p, t], dst_ref=resid.at[p, t],
            send_sem=e_send.at[p, peer], recv_sem=e_recv.at[p, t], device_id=(f, peer), device_id_type=MESH)

    def arrive_resid(peer, p):
        return pltpu.make_async_remote_copy(
            src_ref=resid.at[p, peer], dst_ref=resid.at[p, peer],
            send_sem=e_send.at[p, peer], recv_sem=e_recv.at[p, peer], device_id=(f, peer), device_id_type=MESH)

    spread = ((1, 0), (1, 1), (-1, 0), (-1, 1), (2, 0), (2, 1), (-2, 0), (-2, 1), (0, 1 - x))
    passed = ((-1, 0, 2), (1, 0, -2), (-1, 1, 2), (1, 1, -2), (-2, 0, 2), (2, 1, -2))

    def residue_at(dz, side):
        return lax.rem(odd + dz + 2, 2) * 2 + side

    def send_update(p, n):
        dz, side = spread[n]
        return pltpu.make_async_remote_copy(
            src_ref=update.at[p, residue_at(dz, side)], dst_ref=out.at[0, :, columns_of(f, p), :],
            send_sem=g_send.at[p, n], recv_sem=g_recv.at[p, f],
            device_id=(facet_at(dz, side), t), device_id_type=MESH)

    def pass_on(p, n):
        dz, side, step = passed[n]
        block = out.at[0, :, columns_of(facet_at(dz, side), p), :]
        return pltpu.make_async_remote_copy(
            src_ref=block, dst_ref=block,
            send_sem=f_send.at[p, n], recv_sem=g_recv.at[p, facet_at(dz, side)],
            device_id=(facet_at(step, x), t), device_id_type=MESH)

    def own_update(p):
        return pltpu.make_async_copy(update.at[p, residue_at(0, x)], out.at[0, :, columns_of(f, p), :], g_local.at[p])

    def arrive_update(p, peer):
        return pltpu.make_async_remote_copy(
            src_ref=update.at[p, 0], dst_ref=out.at[0, :, columns_of(peer, p), :],
            send_sem=g_send.at[p, 0], recv_sem=g_recv.at[p, peer],
            device_id=(facet_at(0, 1 - x), t), device_id_type=MESH)

    def relay_updates(p):
        for n in range(6):
            dz, side, _ = passed[n]
            arrive_update(p, facet_at(dz, side)).wait_recv()
            pass_on(p, n).start()

    def forward(p):
        for k in range(4):
            for side in range(2):
                arrive_part(p, k, side).wait_recv()
        arrive_part(p, 4, 1 - x).wait_recv()
        parts[p, 4, x] = mine[:, columns_of(f, p), :]
        for side in range(2):
            same = residue_at(0, side)
            other = residue_at(1, side)
            two = parts[p, 2, side].astype(jnp.float32) + parts[p, 3, side].astype(jnp.float32)
            sums[same] = two + parts[p, 4, side].astype(jnp.float32)
            sums[other] = parts[p, 0, side].astype(jnp.float32) + parts[p, 1, side].astype(jnp.float32)
        for s in range(NSUB):
            cos_phi = phase[0, s]
            sin_phi = phase[1, s]
            for r in range(FROWS):
                a = sums[r, 0]
                b = sums[r, 1]
                row = (s * FROWS + r) * cols
                lhs[row:row + cols, :rows] = (a * cos_phi + b * sin_phi).astype(jnp.bfloat16)
                lhs[row:row + cols, rows:] = (b * cos_phi - a * sin_phi).astype(jnp.bfloat16)
        acc[...] = jnp.dot(lhs[...], table[...], preferred_element_type=jnp.float32)
        for s in range(NSUB):
            total_re = jnp.zeros((cols, half), jnp.float32)
            total_im = jnp.zeros((cols, half), jnp.float32)
            for r in range(FROWS):
                cos_psi, sin_psi = psi(r, s)
                row = (s * FROWS + r) * cols
                re = acc[row:row + cols, :half]
                im = acc[row:row + cols, half:]
                total_re = total_re + re * cos_psi + im * sin_psi
                total_im = total_im + im * cos_psi - re * sin_psi
            total_re = (total_re * scale).astype(jnp.bfloat16)
            total_im = (total_im * scale).astype(jnp.bfloat16)
            for q in range(chunks):
                peer = s * chunks + q
                partial[p, peer, 0] = total_re[:, q * chunk:(q + 1) * chunk]
                partial[p, peer, 1] = total_im[:, q * chunk:(q + 1) * chunk]

        def start_partial(i, _):
            send_partial(strip_peer(i), p).start()
            return 0

        lax.fori_loop(1, ns, start_partial, 0)

    def weigh(p):
        if p == 0:
            @pl.when(apart)
            def _():
                send_vis.wait_recv()
                send_factor.wait_recv()

        def add_partial(i, total):
            peer = strip_peer(i)
            arrive_partial(peer, p).wait_recv()
            return total + partials[p, peer].astype(jnp.float32)

        model = lax.fori_loop(1, ns, add_partial, partial[p, t].astype(jnp.float32))
        mine = slice(p * cols, (p + 1) * cols)
        resid[p, t] = (factor_here[mine][None] * (vis_here[:, mine] - model)).astype(jnp.bfloat16)

        def start_resid(i, _):
            send_resid(strip_peer(i), p).start()
            return 0

        lax.fori_loop(1, ns, start_resid, 0)

    def adjoint(p):
        def wait_resid(i, _):
            arrive_resid(strip_peer(i), p).wait_recv()
            return 0

        lax.fori_loop(1, ns, wait_resid, 0)
        for r in range(FROWS):
            for s in range(NSUB):
                cos_psi, sin_psi = psi(r, s)
                row = (r * NSUB + s) * cols
                for q in range(chunks):
                    g = resid[p, s * chunks + q, 0].astype(jnp.float32)
                    h = resid[p, s * chunks + q, 1].astype(jnp.float32)
                    c = cos_psi[:, q * chunk:(q + 1) * chunk]
                    d = sin_psi[:, q * chunk:(q + 1) * chunk]
                    lhs[row:row + cols, q * chunk:(q + 1) * chunk] = (g * c - h * d).astype(jnp.bfloat16)
                    lhs[row:row + cols, half + q * chunk:half + (q + 1) * chunk] = (h * c + g * d).astype(jnp.bfloat16)
        acc[...] = lax.dot_general(
            lhs[...], table[...], (((1,), (1,)), ((), ())), preferred_element_type=jnp.float32)
        for r in range(FROWS):
            total_re = jnp.zeros((cols, rows), jnp.float32)
            total_im = jnp.zeros((cols, rows), jnp.float32)
            for s in range(NSUB):
                cos_phi = phase[0, s]
                sin_phi = phase[1, s]
                row = (r * NSUB + s) * cols
                a = acc[row:row + cols, :rows]
                b = acc[row:row + cols, rows:]
                total_re = total_re + a * cos_phi - b * sin_phi
                total_im = total_im + b * cos_phi + a * sin_phi
            update[p, r, 0] = (total_re * scale).astype(jnp.bfloat16)
            update[p, r, 1] = (total_im * scale).astype(jnp.bfloat16)

        own_update(p).start()
        for n in range(9):
            send_update(p, n).start()

    with jax.named_scope("transforms"):
        forward(0)
        weigh(0)
        forward(1)
        adjoint(0)
        weigh(1)
        relay_updates(0)
        adjoint(1)
        relay_updates(1)

    with jax.named_scope("drain"):
        for p in range(PASSES):
            def drain_strip(i, _):
                peer = strip_peer(i)
                send_partial(peer, p).wait_send()
                send_resid(peer, p).wait_send()
                return 0

            lax.fori_loop(1, ns, drain_strip, 0)
            for u in range(3):
                for way in range(2):
                    relay(p, way, u).wait_send()
                    joined(p, way, u).wait_send()
                direct(p, u).wait_send()
            for n in range(9):
                send_update(p, n).wait_send()
            for n in range(6):
                pass_on(p, n).wait_send()
            own_update(p).wait()
            arrive_update(p, facet_at(0, 1 - x)).wait_recv()
            for dz, side in ((-2, 1), (2, 0), (3, 0), (3, 1), (-3, 0), (-3, 1), (4, 0), (4, 1)):
                arrive_update(p, facet_at(dz, side)).wait_recv()

        @pl.when(apart)
        def _():
            send_vis.wait_send()
            send_factor.wait_send()


def on_device(nf, ns, facets, offsets, visibilities, weights, mask):
    _, _, columns, rows = facets.shape
    cols = columns // nf // PASSES
    frequencies = visibilities.shape[2] * nf
    half = frequencies // NSUB
    chunk = frequencies // ns
    hbm = pl.BlockSpec(memory_space=pltpu.HBM)
    dma = pltpu.SemaphoreType.DMA
    flops = 2 * 2 * FROWS * NSUB * cols * PASSES * (2 * rows) * (2 * half)
    exchanged = (PASSES, ns, 2, cols, chunk)
    return pl.pallas_call(
        functools.partial(kernel, nf, ns),
        out_shape=jax.ShapeDtypeStruct(facets.shape, jnp.bfloat16),
        in_specs=[hbm] * 5,
        out_specs=hbm,
        scratch_shapes=[
            pltpu.SMEM(offsets.shape, jnp.int32),
            pltpu.VMEM(weights.shape, jnp.float32),
            pltpu.VMEM(mask.shape, jnp.int32),
            pltpu.VMEM((2, columns, rows), jnp.bfloat16),
            pltpu.VMEM((PASSES, 2, 3, 2, cols, rows), jnp.bfloat16),
            pltpu.VMEM((PASSES, 2, 3, 2, cols, rows), jnp.bfloat16),
            pltpu.VMEM((PASSES, 5, 2, 2, cols, rows), jnp.bfloat16),
            pltpu.VMEM((2 * rows, 2 * half), jnp.bfloat16),
            pltpu.VMEM((2, NSUB, 1, rows), jnp.float32),
            pltpu.VMEM((FROWS * NSUB * cols, 2 * max(half, rows)), jnp.bfloat16),
            pltpu.VMEM((FROWS * NSUB * cols, 2 * max(half, rows)), jnp.float32),
            pltpu.VMEM(weights.shape, jnp.float32),
            pltpu.VMEM(visibilities.shape, jnp.float32),
            pltpu.VMEM(weights.shape, jnp.float32),
            pltpu.VMEM(exchanged, jnp.bfloat16),
            pltpu.VMEM(exchanged, jnp.bfloat16),
            pltpu.VMEM(exchanged, jnp.bfloat16),
            pltpu.VMEM((FROWS, 2, cols, rows), jnp.float32),
            pltpu.VMEM((PASSES, FROWS, 2, cols, rows), jnp.bfloat16),
            dma((PASSES, 2, 3)), dma((PASSES, 2, 3)), dma((PASSES, 9)), dma((PASSES, 5, 2)), dma((2,)), dma((2,)),
            dma((PASSES, ns)), dma((PASSES, ns)), dma((PASSES, ns)), dma((PASSES, ns)),
            dma((PASSES, 9)), dma((PASSES, 6)), dma((PASSES, nf)), dma((PASSES,)), dma((5,)),
        ],
        cost_estimate=pl.CostEstimate(flops=flops, bytes_accessed=4 * facets.size, transcendentals=0),
        compiler_params=pltpu.CompilerParams(
            collective_id=0, has_side_effects=True, vmem_limit_bytes=50 * 1024 * 1024),
    )(*(pltpu.with_memory_space_constraint(value, pltpu.HBM) for value in (facets, offsets, visibilities, weights, mask)))


def solution(mesh):
    placed = (
        P("facet", None, None, "strip"),
        P(),
        P(None, "strip", "facet"),
        P("strip", "facet"),
        P("strip", "facet"),
    )
    return jax.shard_map(
        functools.partial(on_device, mesh.shape["facet"], mesh.shape["strip"]),
        mesh=mesh,
        in_specs=placed,
        out_specs=P("facet", None, None, "strip"),
        check_vma=False,
    )
```

```python
import functools
import math

import jax
import jax.numpy as jnp
from jax import lax
from jax.experimental import pallas as pl
from jax.experimental.pallas import tpu as pltpu
from jax.sharding import PartitionSpec as P

NSUB = 4
FROWS = 4
MESH = pl.DeviceIdType.MESH


def turn(count, cells):
    quarter = cells // 4
    shift = quarter.bit_length() - 1
    quadrant = (count + quarter // 2) >> shift
    angle = (count - (quadrant << shift)).astype(jnp.float32) * (2.0 * math.pi / cells)
    square = angle * angle
    sine = angle * (1.0 + square * (-1.0 / 6 + square * (1.0 / 120 + square * (-1.0 / 5040 + square * (1.0 / 362880)))))
    cosine = 1.0 + square * (-0.5 + square * (1.0 / 24 + square * (-1.0 / 720 + square * (1.0 / 40320))))
    odd = (quadrant & 1) == 1
    first = jnp.where(odd, sine, cosine)
    second = jnp.where(odd, cosine, sine)
    cos_value = jnp.where(((quadrant + 1) & 2) == 2, -first, first)
    sin_value = jnp.where((quadrant & 2) == 2, -second, second)
    return cos_value, sin_value


def quarter_turn(count):
    part = count & 3
    sign = jnp.where(part >= 2, -1.0, 1.0)
    even = (part & 1) == 0
    return jnp.where(even, sign, 0.0), jnp.where(even, 0.0, sign)


PASSES = 2


def kernel(
    nf, ns,
    facets, offsets_in, vis, weights_in, mask_in, out,
    offsets, weights, mask, mine, relayed, joint, parts, table, phase, lhs, acc, factor, vis_here, factor_here, partial, partials, resid, sums, update,
    r_send, r_recv, a_send, a_recv, v_send, v_recv, c_send, c_recv, e_send, e_recv, g_send, f_send, g_recv, g_local, local_sem,
):
    f = lax.axis_index("facet")
    t = lax.axis_index("strip")
    cols, rows = parts.shape[4], parts.shape[5]
    cells = FROWS * rows * ns
    half = table.shape[1] // 2
    chunk = partial.shape[4]
    chunks = half // chunk
    scale = 1.0 / math.sqrt(rows * ns)
    start = t * rows
    apart = f != t

    depth = nf // 2
    z = lax.div(f, 2)
    x = lax.rem(f, 2)
    odd = lax.rem(z, 2)

    def facet_at(dz, side):
        return lax.rem(z + dz + depth, depth) * 2 + side

    def strip_peer(i):
        return lax.rem(t + i, ns)

    def columns_of(g, p):
        return pl.ds(pl.multiple_of((g * PASSES + p) * cols, cols), cols)

    barrier = pltpu.get_barrier_semaphore()

    def greet_strip(i, _):
        pl.semaphore_signal(barrier, inc=1, device_id=(f, strip_peer(i)), device_id_type=MESH)
        return 0

    for dz in (1, -1, 2, -2):
        for side in range(2):
            pl.semaphore_signal(barrier, inc=1, device_id=(facet_at(dz, side), t), device_id_type=MESH)
    pl.semaphore_signal(barrier, inc=1, device_id=(facet_at(0, 1 - x), t), device_id_type=MESH)
    lax.fori_loop(1, ns, greet_strip, 0)

    @pl.when(apart)
    def _():
        pl.semaphore_signal(barrier, inc=1, device_id=(t, f), device_id_type=MESH)

    get_offsets = pltpu.make_async_copy(offsets_in, offsets, local_sem.at[0])
    get_weights = pltpu.make_async_copy(weights_in, weights, local_sem.at[1])
    get_mask = pltpu.make_async_copy(mask_in, mask, local_sem.at[2])
    get_vis = pltpu.make_async_copy(vis, vis_here, local_sem.at[3])
    get_offsets.start()
    get_weights.start()
    get_mask.start()
    get_mine = pltpu.make_async_copy(facets.at[0], mine, local_sem.at[4])
    get_mine.start()

    pl.semaphore_wait(barrier, 9 + ns - 1 + apart.astype(jnp.int32))

    routes = (((1, 0), (1, 1), (2, 0)), ((-1, 0), (-1, 1), (-2, 1)))
    place = {1: 0, -1: 1, 2: 2, -2: 3, 0: 4}

    def relay(p, way, u):
        step = 2 - 4 * way
        dz, side = routes[way][u]
        return pltpu.make_async_remote_copy(
            src_ref=mine.at[:, columns_of(facet_at(dz + step, side), p), :], dst_ref=relayed.at[p, way, u],
            send_sem=r_send.at[p, way, u], recv_sem=r_recv.at[p, way, u],
            device_id=(facet_at(step, x), t), device_id_type=MESH)

    def joined(p, way, u):
        dz, side = routes[way][u]
        return pltpu.make_async_remote_copy(
            src_ref=joint.at[p, way, u], dst_ref=parts.at[p, place[dz], x],
            send_sem=a_send.at[p, 3 * way + u], recv_sem=a_recv.at[p, place[dz], x],
            device_id=(facet_at(dz, side), t), device_id_type=MESH)

    def direct(p, n):
        dz, side = ((2, 1), (-2, 0), (0, 1 - x))[n]
        peer = facet_at(dz, side)
        return pltpu.make_async_remote_copy(
            src_ref=mine.at[:, columns_of(peer, p), :], dst_ref=parts.at[p, place[dz], x],
            send_sem=a_send.at[p, 6 + n], recv_sem=a_recv.at[p, place[dz], x],
            device_id=(peer, t), device_id_type=MESH)

    def arrive_part(p, k, side):
        return pltpu.make_async_remote_copy(
            src_ref=parts.at[p, k, side], dst_ref=parts.at[p, k, side],
            send_sem=a_send.at[p, 0], recv_sem=a_recv.at[p, k, side],
            device_id=(facet_at(0, 1 - x), t), device_id_type=MESH)

    def start_relays(p):
        for u in range(3):
            for way in range(2):
                relay(p, way, u).start()
        for n in range(3):
            direct(p, n).start()

    def join(p):
        for u in range(3):
            for way in range(2):
                relay(p, way, u).wait_recv()
                own = mine[:, columns_of(facet_at(*routes[way][u]), p), :]
                joint[p, way, u] = (relayed[p, way, u].astype(jnp.float32) + own.astype(jnp.float32)).astype(jnp.bfloat16)
                joined(p, way, u).start()
                if p + 1 < PASSES:
                    relay(p + 1, way, u).start()
        if p + 1 < PASSES:
            for n in range(3):
                direct(p + 1, n).start()

    get_mine.wait()
    start_relays(0)
    get_weights.wait()
    get_mask.wait()
    factor[...] = weights[...] * mask[...].astype(jnp.float32)
    send_vis = pltpu.make_async_remote_copy(
        src_ref=vis, dst_ref=vis_here, send_sem=v_send.at[0], recv_sem=v_recv.at[0], device_id=(t, f), device_id_type=MESH)
    send_factor = pltpu.make_async_remote_copy(
        src_ref=factor, dst_ref=factor_here, send_sem=v_send.at[1], recv_sem=v_recv.at[1], device_id=(t, f), device_id_type=MESH)

    @pl.when(apart)
    def _():
        send_vis.start()
        send_factor.start()

    @pl.when(jnp.logical_not(apart))
    def _():
        get_vis.start()
        factor_here[...] = factor[...]
        get_vis.wait()

    get_offsets.wait()

    with jax.named_scope("tables"):
        block = min(32, rows)

        def fill(i, _):
            base = pl.multiple_of(i * block, block)
            row = start + base + lax.broadcasted_iota(jnp.int32, (block, half), 0)
            j = lax.broadcasted_iota(jnp.int32, (block, half), 1)
            cos_value, sin_value = turn((row * j) & (cells - 1), cells)
            low = pl.ds(base, block)
            high = pl.ds(pl.multiple_of(rows + base, block), block)
            cos_value = cos_value.astype(jnp.bfloat16)
            table[low, :half] = cos_value
            table[high, half:] = cos_value
            table[low, half:] = (-sin_value).astype(jnp.bfloat16)
            table[high, :half] = sin_value.astype(jnp.bfloat16)
            return 0

        lax.fori_loop(0, rows // block, fill, 0)
        for s in range(NSUB):
            row = start + lax.broadcasted_iota(jnp.int32, (1, rows), 1)
            cos_value, sin_value = turn((row * offsets[s]) & (cells - 1), cells)
            phase[0, s] = cos_value
            phase[1, s] = sin_value

    for p in range(PASSES):
        join(p)

    def psi(r, s):
        j = lax.broadcasted_iota(jnp.int32, (1, half), 1)
        return quarter_turn((offsets[s] + j) * (r + 2))

    def send_partial(peer, p):
        return pltpu.make_async_remote_copy(
            src_ref=partial.at[p, peer], dst_ref=partials.at[p, t],
            send_sem=c_send.at[p, peer], recv_sem=c_recv.at[p, t], device_id=(f, peer), device_id_type=MESH)

    def arrive_partial(peer, p):
        return pltpu.make_async_remote_copy(
            src_ref=partial.at[p, peer], dst_ref=partials.at[p, peer],
            send_sem=c_send.at[p, peer], recv_sem=c_recv.at[p, peer], device_id=(f, peer), device_id_type=MESH)

    def send_resid(peer, p):
        return pltpu.make_async_remote_copy(
            src_ref=resid.at[p, t], dst_ref=resid.at[p, t],
            send_sem=e_send.at[p, peer], recv_sem=e_recv.at[p, t], device_id=(f, peer), device_id_type=MESH)

    def arrive_resid(peer, p):
        return pltpu.make_async_remote_copy(
            src_ref=resid.at[p, peer], dst_ref=resid.at[p, peer],
            send_sem=e_send.at[p, peer], recv_sem=e_recv.at[p, peer], device_id=(f, peer), device_id_type=MESH)

    spread = ((1, 0), (1, 1), (-1, 0), (-1, 1), (2, 0), (2, 1), (-2, 0), (-2, 1), (0, 1 - x))
    passed = ((-1, 0, 2), (1, 0, -2), (-1, 1, 2), (1, 1, -2), (-2, 0, 2), (2, 1, -2))

    def residue_at(dz, side):
        return lax.rem(odd + dz + 2, 2) * 2 + side

    def slot_of(dz, side):
        return (0 if dz in (1, -1) else 2) + side

    def send_update(p, n):
        dz, side = spread[n]
        return pltpu.make_async_remote_copy(
            src_ref=update.at[p, slot_of(dz, side)], dst_ref=out.at[0, :, columns_of(f, p), :],
            send_sem=g_send.at[p, n], recv_sem=g_recv.at[p, f],
            device_id=(facet_at(dz, side), t), device_id_type=MESH)

    def pass_on(p, n):
        dz, side, step = passed[n]
        block = out.at[0, :, columns_of(facet_at(dz, side), p), :]
        return pltpu.make_async_remote_copy(
            src_ref=block, dst_ref=block,
            send_sem=f_send.at[p, n], recv_sem=g_recv.at[p, facet_at(dz, side)],
            device_id=(facet_at(step, x), t), device_id_type=MESH)

    def own_update(p):
        return pltpu.make_async_copy(update.at[p, slot_of(0, x)], out.at[0, :, columns_of(f, p), :], g_local.at[p])

    def arrive_update(p, peer):
        return pltpu.make_async_remote_copy(
            src_ref=update.at[p, 0], dst_ref=out.at[0, :, columns_of(peer, p), :],
            send_sem=g_send.at[p, 0], recv_sem=g_recv.at[p, peer],
            device_id=(facet_at(0, 1 - x), t), device_id_type=MESH)

    def relay_updates(p):
        for n in range(6):
            dz, side, _ = passed[n]
            arrive_update(p, facet_at(dz, side)).wait_recv()
            pass_on(p, n).start()

    def forward(p):
        for k in range(4):
            for side in range(2):
                arrive_part(p, k, side).wait_recv()
        arrive_part(p, 4, 1 - x).wait_recv()
        parts[p, 4, x] = mine[:, columns_of(f, p), :]
        for side in range(2):
            same = residue_at(0, side)
            other = residue_at(1, side)
            two = parts[p, 2, side].astype(jnp.float32) + parts[p, 3, side].astype(jnp.float32)
            sums[same] = two + parts[p, 4, side].astype(jnp.float32)
            sums[other] = parts[p, 0, side].astype(jnp.float32) + parts[p, 1, side].astype(jnp.float32)
        for s in range(NSUB):
            cos_phi = phase[0, s]
            sin_phi = phase[1, s]
            for r in range(FROWS):
                a = sums[r, 0]
                b = sums[r, 1]
                row = (s * FROWS + r) * cols
                lhs[row:row + cols, :rows] = (a * cos_phi + b * sin_phi).astype(jnp.bfloat16)
                lhs[row:row + cols, rows:] = (b * cos_phi - a * sin_phi).astype(jnp.bfloat16)
        acc[...] = jnp.dot(lhs[...], table[...], preferred_element_type=jnp.float32)
        for s in range(NSUB):
            total_re = jnp.zeros((cols, half), jnp.float32)
            total_im = jnp.zeros((cols, half), jnp.float32)
            for r in range(FROWS):
                cos_psi, sin_psi = psi(r, s)
                row = (s * FROWS + r) * cols
                re = acc[row:row + cols, :half]
                im = acc[row:row + cols, half:]
                total_re = total_re + re * cos_psi + im * sin_psi
                total_im = total_im + im * cos_psi - re * sin_psi
            total_re = (total_re * scale).astype(jnp.bfloat16)
            total_im = (total_im * scale).astype(jnp.bfloat16)
            for q in range(chunks):
                peer = s * chunks + q
                partial[p, peer, 0] = total_re[:, q * chunk:(q + 1) * chunk]
                partial[p, peer, 1] = total_im[:, q * chunk:(q + 1) * chunk]

                @pl.when(peer != t)
                def _():
                    send_partial(peer, p).start()

    def weigh(p):
        if p == 0:
            @pl.when(apart)
            def _():
                send_vis.wait_recv()
                send_factor.wait_recv()

        def add_partial(i, total):
            peer = strip_peer(i)
            arrive_partial(peer, p).wait_recv()
            return total + partials[p, peer].astype(jnp.float32)

        model = lax.fori_loop(1, ns, add_partial, partial[p, t].astype(jnp.float32))
        mine = slice(p * cols, (p + 1) * cols)
        resid[p, t] = (factor_here[mine][None] * (vis_here[:, mine] - model)).astype(jnp.bfloat16)

        def start_resid(i, _):
            send_resid(strip_peer(i), p).start()
            return 0

        lax.fori_loop(1, ns, start_resid, 0)

    def adjoint(p):
        def wait_resid(i, _):
            arrive_resid(strip_peer(i), p).wait_recv()
            return 0

        lax.fori_loop(1, ns, wait_resid, 0)
        for r in range(FROWS):
            for s in range(NSUB):
                cos_psi, sin_psi = psi(residue_at(1 - r // 2, r % 2), s)
                row = (r * NSUB + s) * cols
                for q in range(chunks):
                    g = resid[p, s * chunks + q, 0].astype(jnp.float32)
                    h = resid[p, s * chunks + q, 1].astype(jnp.float32)
                    c = cos_psi[:, q * chunk:(q + 1) * chunk]
                    d = sin_psi[:, q * chunk:(q + 1) * chunk]
                    lhs[row:row + cols, q * chunk:(q + 1) * chunk] = (g * c - h * d).astype(jnp.bfloat16)
                    lhs[row:row + cols, half + q * chunk:half + (q + 1) * chunk] = (h * c + g * d).astype(jnp.bfloat16)
        acc[...] = lax.dot_general(
            lhs[...], table[...], (((1,), (1,)), ((), ())), preferred_element_type=jnp.float32)
        for r in range(FROWS):
            total_re = jnp.zeros((cols, rows), jnp.float32)
            total_im = jnp.zeros((cols, rows), jnp.float32)
            for s in range(NSUB):
                cos_phi = phase[0, s]
                sin_phi = phase[1, s]
                row = (r * NSUB + s) * cols
                a = acc[row:row + cols, :rows]
                b = acc[row:row + cols, rows:]
                total_re = total_re + a * cos_phi - b * sin_phi
                total_im = total_im + b * cos_phi + a * sin_phi
            update[p, r, 0] = (total_re * scale).astype(jnp.bfloat16)
            update[p, r, 1] = (total_im * scale).astype(jnp.bfloat16)
            for n in ((0, 2), (1, 3), (4, 6), (5, 7))[r]:
                send_update(p, n).start()

        send_update(p, 8).start()
        own_update(p).start()

    with jax.named_scope("transforms"):
        forward(0)
        weigh(0)
        forward(1)
        adjoint(0)
        weigh(1)
        relay_updates(0)
        adjoint(1)
        relay_updates(1)

    with jax.named_scope("drain"):
        for p in range(PASSES):
            def drain_strip(i, _):
                peer = strip_peer(i)
                send_partial(peer, p).wait_send()
                send_resid(peer, p).wait_send()
                return 0

            lax.fori_loop(1, ns, drain_strip, 0)
            for u in range(3):
                for way in range(2):
                    relay(p, way, u).wait_send()
                    joined(p, way, u).wait_send()
                direct(p, u).wait_send()
            for n in range(9):
                send_update(p, n).wait_send()
            for n in range(6):
                pass_on(p, n).wait_send()
            own_update(p).wait()
            arrive_update(p, facet_at(0, 1 - x)).wait_recv()
            for dz, side in ((-2, 1), (2, 0), (3, 0), (3, 1), (-3, 0), (-3, 1), (4, 0), (4, 1)):
                arrive_update(p, facet_at(dz, side)).wait_recv()

        @pl.when(apart)
        def _():
            send_vis.wait_send()
            send_factor.wait_send()


def on_device(nf, ns, facets, offsets, visibilities, weights, mask):
    _, _, columns, rows = facets.shape
    cols = columns // nf // PASSES
    frequencies = visibilities.shape[2] * nf
    half = frequencies // NSUB
    chunk = frequencies // ns
    hbm = pl.BlockSpec(memory_space=pltpu.HBM)
    dma = pltpu.SemaphoreType.DMA
    flops = 2 * 2 * FROWS * NSUB * cols * PASSES * (2 * rows) * (2 * half)
    exchanged = (PASSES, ns, 2, cols, chunk)
    return pl.pallas_call(
        functools.partial(kernel, nf, ns),
        out_shape=jax.ShapeDtypeStruct(facets.shape, jnp.bfloat16),
        in_specs=[hbm] * 5,
        out_specs=hbm,
        scratch_shapes=[
            pltpu.SMEM(offsets.shape, jnp.int32),
            pltpu.VMEM(weights.shape, jnp.float32),
            pltpu.VMEM(mask.shape, jnp.int32),
            pltpu.VMEM((2, columns, rows), jnp.bfloat16),
            pltpu.VMEM((PASSES, 2, 3, 2, cols, rows), jnp.bfloat16),
            pltpu.VMEM((PASSES, 2, 3, 2, cols, rows), jnp.bfloat16),
            pltpu.VMEM((PASSES, 5, 2, 2, cols, rows), jnp.bfloat16),
            pltpu.VMEM((2 * rows, 2 * half), jnp.bfloat16),
            pltpu.VMEM((2, NSUB, 1, rows), jnp.float32),
            pltpu.VMEM((FROWS * NSUB * cols, 2 * max(half, rows)), jnp.bfloat16),
            pltpu.VMEM((FROWS * NSUB * cols, 2 * max(half, rows)), jnp.float32),
            pltpu.VMEM(weights.shape, jnp.float32),
            pltpu.VMEM(visibilities.shape, jnp.float32),
            pltpu.VMEM(weights.shape, jnp.float32),
            pltpu.VMEM(exchanged, jnp.bfloat16),
            pltpu.VMEM(exchanged, jnp.bfloat16),
            pltpu.VMEM(exchanged, jnp.bfloat16),
            pltpu.VMEM((FROWS, 2, cols, rows), jnp.float32),
            pltpu.VMEM((PASSES, FROWS, 2, cols, rows), jnp.bfloat16),
            dma((PASSES, 2, 3)), dma((PASSES, 2, 3)), dma((PASSES, 9)), dma((PASSES, 5, 2)), dma((2,)), dma((2,)),
            dma((PASSES, ns)), dma((PASSES, ns)), dma((PASSES, ns)), dma((PASSES, ns)),
            dma((PASSES, 9)), dma((PASSES, 6)), dma((PASSES, nf)), dma((PASSES,)), dma((5,)),
        ],
        cost_estimate=pl.CostEstimate(flops=flops, bytes_accessed=4 * facets.size, transcendentals=0),
        compiler_params=pltpu.CompilerParams(
            collective_id=0, has_side_effects=True, vmem_limit_bytes=50 * 1024 * 1024),
    )(*(pltpu.with_memory_space_constraint(value, pltpu.HBM) for value in (facets, offsets, visibilities, weights, mask)))


def solution(mesh):
    placed = (
        P("facet", None, None, "strip"),
        P(),
        P(None, "strip", "facet"),
        P("strip", "facet"),
        P("strip", "facet"),
    )
    return jax.shard_map(
        functools.partial(on_device, mesh.shape["facet"], mesh.shape["strip"]),
        mesh=mesh,
        in_specs=placed,
        out_specs=P("facet", None, None, "strip"),
        check_vma=False,
    )
```

```python
import functools
import math

import jax
import jax.numpy as jnp
from jax import lax
from jax.experimental import pallas as pl
from jax.experimental.pallas import tpu as pltpu
from jax.sharding import PartitionSpec as P

NSUB = 4
FROWS = 4
MESH = pl.DeviceIdType.MESH


def turn(count, cells):
    quarter = cells // 4
    shift = quarter.bit_length() - 1
    quadrant = (count + quarter // 2) >> shift
    angle = (count - (quadrant << shift)).astype(jnp.float32) * (2.0 * math.pi / cells)
    square = angle * angle
    sine = angle * (1.0 + square * (-1.0 / 6 + square * (1.0 / 120 + square * (-1.0 / 5040 + square * (1.0 / 362880)))))
    cosine = 1.0 + square * (-0.5 + square * (1.0 / 24 + square * (-1.0 / 720 + square * (1.0 / 40320))))
    odd = (quadrant & 1) == 1
    first = jnp.where(odd, sine, cosine)
    second = jnp.where(odd, cosine, sine)
    cos_value = jnp.where(((quadrant + 1) & 2) == 2, -first, first)
    sin_value = jnp.where((quadrant & 2) == 2, -second, second)
    return cos_value, sin_value


def quarter_turn(count):
    part = count & 3
    sign = jnp.where(part >= 2, -1.0, 1.0)
    even = (part & 1) == 0
    return jnp.where(even, sign, 0.0), jnp.where(even, 0.0, sign)


PASSES = 2


def kernel(
    nf, ns,
    facets, offsets_in, vis, weights_in, mask_in, out,
    offsets, weights, mask, mine, relayed, joint, parts, table, phase, lhs, acc, factor, vis_here, factor_here, partial, partials, resid, sums, update,
    r_send, r_recv, a_send, a_recv, v_send, v_recv, c_send, c_recv, e_send, e_recv, g_send, f_send, g_recv, g_local, local_sem,
):
    f = lax.axis_index("facet")
    t = lax.axis_index("strip")
    cols, rows = parts.shape[4], parts.shape[5]
    cells = FROWS * rows * ns
    half = table.shape[1] // 2
    chunk = partial.shape[4]
    chunks = half // chunk
    scale = 1.0 / math.sqrt(rows * ns)
    start = t * rows
    apart = f != t

    depth = nf // 2
    z = lax.div(f, 2)
    x = lax.rem(f, 2)
    odd = lax.rem(z, 2)

    def facet_at(dz, side):
        return lax.rem(z + dz + depth, depth) * 2 + side

    def strip_peer(i):
        return lax.rem(t + i, ns)

    def columns_of(g, p):
        return pl.ds(pl.multiple_of((g * PASSES + p) * cols, cols), cols)

    barrier = pltpu.get_barrier_semaphore()

    def greet_strip(i, _):
        pl.semaphore_signal(barrier, inc=1, device_id=(f, strip_peer(i)), device_id_type=MESH)
        return 0

    for dz in (1, -1, 2, -2):
        for side in range(2):
            pl.semaphore_signal(barrier, inc=1, device_id=(facet_at(dz, side), t), device_id_type=MESH)
    pl.semaphore_signal(barrier, inc=1, device_id=(facet_at(0, 1 - x), t), device_id_type=MESH)
    lax.fori_loop(1, ns, greet_strip, 0)

    @pl.when(apart)
    def _():
        pl.semaphore_signal(barrier, inc=1, device_id=(t, f), device_id_type=MESH)

    get_offsets = pltpu.make_async_copy(offsets_in, offsets, local_sem.at[0])
    get_weights = pltpu.make_async_copy(weights_in, weights, local_sem.at[1])
    get_mask = pltpu.make_async_copy(mask_in, mask, local_sem.at[2])
    get_vis = pltpu.make_async_copy(vis, vis_here, local_sem.at[3])
    get_offsets.start()
    get_weights.start()
    get_mask.start()
    get_mine = pltpu.make_async_copy(facets.at[0], mine, local_sem.at[4])
    get_mine.start()

    pl.semaphore_wait(barrier, 9 + ns - 1 + apart.astype(jnp.int32))

    routes = (((1, 0), (1, 1), (2, 0)), ((-1, 0), (-1, 1), (-2, 1)))
    place = {1: 0, -1: 1, 2: 2, -2: 3, 0: 4}

    def relay(p, way, u):
        step = 2 - 4 * way
        dz, side = routes[way][u]
        return pltpu.make_async_remote_copy(
            src_ref=mine.at[:, columns_of(facet_at(dz + step, side), p), :], dst_ref=relayed.at[p, way, u],
            send_sem=r_send.at[p, way, u], recv_sem=r_recv.at[p, way, u],
            device_id=(facet_at(step, x), t), device_id_type=MESH)

    def joined(p, way, u):
        dz, side = routes[way][u]
        return pltpu.make_async_remote_copy(
            src_ref=joint.at[p, way, u], dst_ref=parts.at[p, place[dz], x],
            send_sem=a_send.at[p, 3 * way + u], recv_sem=a_recv.at[p, place[dz], x],
            device_id=(facet_at(dz, side), t), device_id_type=MESH)

    def direct(p, n):
        dz, side = ((2, 1), (-2, 0), (0, 1 - x))[n]
        peer = facet_at(dz, side)
        return pltpu.make_async_remote_copy(
            src_ref=mine.at[:, columns_of(peer, p), :], dst_ref=parts.at[p, place[dz], x],
            send_sem=a_send.at[p, 6 + n], recv_sem=a_recv.at[p, place[dz], x],
            device_id=(peer, t), device_id_type=MESH)

    def arrive_part(p, k, side):
        return pltpu.make_async_remote_copy(
            src_ref=parts.at[p, k, side], dst_ref=parts.at[p, k, side],
            send_sem=a_send.at[p, 0], recv_sem=a_recv.at[p, k, side],
            device_id=(facet_at(0, 1 - x), t), device_id_type=MESH)

    def start_relays(p):
        for u in range(3):
            for way in range(2):
                relay(p, way, u).start()
        for n in range(3):
            direct(p, n).start()

    def join(p):
        for u in range(3):
            for way in range(2):
                relay(p, way, u).wait_recv()
                own = mine[:, columns_of(facet_at(*routes[way][u]), p), :]
                joint[p, way, u] = (relayed[p, way, u].astype(jnp.float32) + own.astype(jnp.float32)).astype(jnp.bfloat16)
                joined(p, way, u).start()
                if p + 1 < PASSES:
                    relay(p + 1, way, u).start()
        if p + 1 < PASSES:
            for n in range(3):
                direct(p + 1, n).start()

    get_mine.wait()
    start_relays(0)
    get_weights.wait()
    get_mask.wait()
    factor[...] = weights[...] * mask[...].astype(jnp.float32)
    send_vis = pltpu.make_async_remote_copy(
        src_ref=vis, dst_ref=vis_here, send_sem=v_send.at[0], recv_sem=v_recv.at[0], device_id=(t, f), device_id_type=MESH)
    send_factor = pltpu.make_async_remote_copy(
        src_ref=factor, dst_ref=factor_here, send_sem=v_send.at[1], recv_sem=v_recv.at[1], device_id=(t, f), device_id_type=MESH)

    @pl.when(jnp.logical_not(apart))
    def _():
        get_vis.start()
        factor_here[...] = factor[...]
        get_vis.wait()

    get_offsets.wait()

    with jax.named_scope("tables"):
        block = min(32, rows)

        def fill(i, _):
            base = pl.multiple_of(i * block, block)
            row = start + base + lax.broadcasted_iota(jnp.int32, (block, half), 0)
            j = lax.broadcasted_iota(jnp.int32, (block, half), 1)
            cos_value, sin_value = turn((row * j) & (cells - 1), cells)
            low = pl.ds(base, block)
            high = pl.ds(pl.multiple_of(rows + base, block), block)
            cos_value = cos_value.astype(jnp.bfloat16)
            table[low, :half] = cos_value
            table[high, half:] = cos_value
            table[low, half:] = (-sin_value).astype(jnp.bfloat16)
            table[high, :half] = sin_value.astype(jnp.bfloat16)
            return 0

        lax.fori_loop(0, rows // block, fill, 0)
        for s in range(NSUB):
            row = start + lax.broadcasted_iota(jnp.int32, (1, rows), 1)
            cos_value, sin_value = turn((row * offsets[s]) & (cells - 1), cells)
            phase[0, s] = cos_value
            phase[1, s] = sin_value

    join(0)

    @pl.when(apart)
    def _():
        send_vis.start()
        send_factor.start()

    join(1)

    def psi(r, s):
        j = lax.broadcasted_iota(jnp.int32, (1, half), 1)
        return quarter_turn((offsets[s] + j) * (r + 2))

    def send_partial(peer, p):
        return pltpu.make_async_remote_copy(
            src_ref=partial.at[p, peer], dst_ref=partials.at[p, t],
            send_sem=c_send.at[p, peer], recv_sem=c_recv.at[p, t], device_id=(f, peer), device_id_type=MESH)

    def arrive_partial(peer, p):
        return pltpu.make_async_remote_copy(
            src_ref=partial.at[p, peer], dst_ref=partials.at[p, peer],
            send_sem=c_send.at[p, peer], recv_sem=c_recv.at[p, peer], device_id=(f, peer), device_id_type=MESH)

    def send_resid(peer, p):
        return pltpu.make_async_remote_copy(
            src_ref=resid.at[p, t], dst_ref=resid.at[p, t],
            send_sem=e_send.at[p, peer], recv_sem=e_recv.at[p, t], device_id=(f, peer), device_id_type=MESH)

    def arrive_resid(peer, p):
        return pltpu.make_async_remote_copy(
            src_ref=resid.at[p, peer], dst_ref=resid.at[p, peer],
            send_sem=e_send.at[p, peer], recv_sem=e_recv.at[p, peer], device_id=(f, peer), device_id_type=MESH)

    spread = ((1, 0), (1, 1), (-1, 0), (-1, 1), (2, 0), (2, 1), (-2, 0), (-2, 1), (0, 1 - x))
    passed = ((-1, 0, 2), (1, 0, -2), (-1, 1, 2), (1, 1, -2), (-2, 0, 2), (2, 1, -2))

    def residue_at(dz, side):
        return lax.rem(odd + dz + 2, 2) * 2 + side

    def slot_of(dz, side):
        return (0 if dz in (1, -1) else 2) + side

    def send_update(p, n):
        dz, side = spread[n]
        return pltpu.make_async_remote_copy(
            src_ref=update.at[p, slot_of(dz, side)], dst_ref=out.at[0, :, columns_of(f, p), :],
            send_sem=g_send.at[p, n], recv_sem=g_recv.at[p, f],
            device_id=(facet_at(dz, side), t), device_id_type=MESH)

    def pass_on(p, n):
        dz, side, step = passed[n]
        block = out.at[0, :, columns_of(facet_at(dz, side), p), :]
        return pltpu.make_async_remote_copy(
            src_ref=block, dst_ref=block,
            send_sem=f_send.at[p, n], recv_sem=g_recv.at[p, facet_at(dz, side)],
            device_id=(facet_at(step, x), t), device_id_type=MESH)

    def own_update(p):
        return pltpu.make_async_copy(update.at[p, slot_of(0, x)], out.at[0, :, columns_of(f, p), :], g_local.at[p])

    def arrive_update(p, peer):
        return pltpu.make_async_remote_copy(
            src_ref=update.at[p, 0], dst_ref=out.at[0, :, columns_of(peer, p), :],
            send_sem=g_send.at[p, 0], recv_sem=g_recv.at[p, peer],
            device_id=(facet_at(0, 1 - x), t), device_id_type=MESH)

    def relay_updates(p):
        for n in range(6):
            dz, side, _ = passed[n]
            arrive_update(p, facet_at(dz, side)).wait_recv()
            pass_on(p, n).start()

    def forward(p):
        for k in range(4):
            for side in range(2):
                arrive_part(p, k, side).wait_recv()
        arrive_part(p, 4, 1 - x).wait_recv()
        parts[p, 4, x] = mine[:, columns_of(f, p), :]
        for side in range(2):
            same = residue_at(0, side)
            other = residue_at(1, side)
            two = parts[p, 2, side].astype(jnp.float32) + parts[p, 3, side].astype(jnp.float32)
            sums[same] = two + parts[p, 4, side].astype(jnp.float32)
            sums[other] = parts[p, 0, side].astype(jnp.float32) + parts[p, 1, side].astype(jnp.float32)
        for s in range(NSUB):
            cos_phi = phase[0, s]
            sin_phi = phase[1, s]
            for r in range(FROWS):
                a = sums[r, 0]
                b = sums[r, 1]
                row = (s * FROWS + r) * cols
                lhs[row:row + cols, :rows] = (a * cos_phi + b * sin_phi).astype(jnp.bfloat16)
                lhs[row:row + cols, rows:] = (b * cos_phi - a * sin_phi).astype(jnp.bfloat16)
        acc[...] = jnp.dot(lhs[...], table[...], preferred_element_type=jnp.float32)
        for s in range(NSUB):
            total_re = jnp.zeros((cols, half), jnp.float32)
            total_im = jnp.zeros((cols, half), jnp.float32)
            for r in range(FROWS):
                cos_psi, sin_psi = psi(r, s)
                row = (s * FROWS + r) * cols
                re = acc[row:row + cols, :half]
                im = acc[row:row + cols, half:]
                total_re = total_re + re * cos_psi + im * sin_psi
                total_im = total_im + im * cos_psi - re * sin_psi
            total_re = (total_re * scale).astype(jnp.bfloat16)
            total_im = (total_im * scale).astype(jnp.bfloat16)
            for q in range(chunks):
                peer = s * chunks + q
                partial[p, peer, 0] = total_re[:, q * chunk:(q + 1) * chunk]
                partial[p, peer, 1] = total_im[:, q * chunk:(q + 1) * chunk]

                @pl.when(peer != t)
                def _():
                    send_partial(peer, p).start()

    def weigh(p):
        if p == 0:
            @pl.when(apart)
            def _():
                send_vis.wait_recv()
                send_factor.wait_recv()

        def add_partial(i, total):
            peer = strip_peer(i)
            arrive_partial(peer, p).wait_recv()
            return total + partials[p, peer].astype(jnp.float32)

        model = lax.fori_loop(1, ns, add_partial, partial[p, t].astype(jnp.float32))
        mine = slice(p * cols, (p + 1) * cols)
        resid[p, t] = (factor_here[mine][None] * (vis_here[:, mine] - model)).astype(jnp.bfloat16)

        def start_resid(i, _):
            send_resid(strip_peer(i), p).start()
            return 0

        lax.fori_loop(1, ns, start_resid, 0)

    def adjoint(p):
        def wait_resid(i, _):
            arrive_resid(strip_peer(i), p).wait_recv()
            return 0

        lax.fori_loop(1, ns, wait_resid, 0)
        for r in range(FROWS):
            for s in range(NSUB):
                cos_psi, sin_psi = psi(residue_at(1 - r // 2, r % 2), s)
                row = (r * NSUB + s) * cols
                for q in range(chunks):
                    g = resid[p, s * chunks + q, 0].astype(jnp.float32)
                    h = resid[p, s * chunks + q, 1].astype(jnp.float32)
                    c = cos_psi[:, q * chunk:(q + 1) * chunk]
                    d = sin_psi[:, q * chunk:(q + 1) * chunk]
                    lhs[row:row + cols, q * chunk:(q + 1) * chunk] = (g * c - h * d).astype(jnp.bfloat16)
                    lhs[row:row + cols, half + q * chunk:half + (q + 1) * chunk] = (h * c + g * d).astype(jnp.bfloat16)
        acc[...] = lax.dot_general(
            lhs[...], table[...], (((1,), (1,)), ((), ())), preferred_element_type=jnp.float32)
        for r in range(FROWS):
            total_re = jnp.zeros((cols, rows), jnp.float32)
            total_im = jnp.zeros((cols, rows), jnp.float32)
            for s in range(NSUB):
                cos_phi = phase[0, s]
                sin_phi = phase[1, s]
                row = (r * NSUB + s) * cols
                a = acc[row:row + cols, :rows]
                b = acc[row:row + cols, rows:]
                total_re = total_re + a * cos_phi - b * sin_phi
                total_im = total_im + b * cos_phi + a * sin_phi
            update[p, r, 0] = (total_re * scale).astype(jnp.bfloat16)
            update[p, r, 1] = (total_im * scale).astype(jnp.bfloat16)
            for n in ((0, 2), (1, 3), (4, 6), (5, 7))[r]:
                send_update(p, n).start()

        send_update(p, 8).start()
        own_update(p).start()

    with jax.named_scope("transforms"):
        forward(0)
        weigh(0)
        forward(1)
        adjoint(0)
        weigh(1)
        relay_updates(0)
        adjoint(1)
        relay_updates(1)

    with jax.named_scope("drain"):
        for p in range(PASSES):
            def drain_strip(i, _):
                peer = strip_peer(i)
                send_partial(peer, p).wait_send()
                send_resid(peer, p).wait_send()
                return 0

            lax.fori_loop(1, ns, drain_strip, 0)
            for u in range(3):
                for way in range(2):
                    relay(p, way, u).wait_send()
                    joined(p, way, u).wait_send()
                direct(p, u).wait_send()
            for n in range(9):
                send_update(p, n).wait_send()
            for n in range(6):
                pass_on(p, n).wait_send()
            own_update(p).wait()
            arrive_update(p, facet_at(0, 1 - x)).wait_recv()
            for dz, side in ((-2, 1), (2, 0), (3, 0), (3, 1), (-3, 0), (-3, 1), (4, 0), (4, 1)):
                arrive_update(p, facet_at(dz, side)).wait_recv()

        @pl.when(apart)
        def _():
            send_vis.wait_send()
            send_factor.wait_send()


def on_device(nf, ns, facets, offsets, visibilities, weights, mask):
    _, _, columns, rows = facets.shape
    cols = columns // nf // PASSES
    frequencies = visibilities.shape[2] * nf
    half = frequencies // NSUB
    chunk = frequencies // ns
    hbm = pl.BlockSpec(memory_space=pltpu.HBM)
    dma = pltpu.SemaphoreType.DMA
    flops = 2 * 2 * FROWS * NSUB * cols * PASSES * (2 * rows) * (2 * half)
    exchanged = (PASSES, ns, 2, cols, chunk)
    return pl.pallas_call(
        functools.partial(kernel, nf, ns),
        out_shape=jax.ShapeDtypeStruct(facets.shape, jnp.bfloat16),
        in_specs=[hbm] * 5,
        out_specs=hbm,
        scratch_shapes=[
            pltpu.SMEM(offsets.shape, jnp.int32),
            pltpu.VMEM(weights.shape, jnp.float32),
            pltpu.VMEM(mask.shape, jnp.int32),
            pltpu.VMEM((2, columns, rows), jnp.bfloat16),
            pltpu.VMEM((PASSES, 2, 3, 2, cols, rows), jnp.bfloat16),
            pltpu.VMEM((PASSES, 2, 3, 2, cols, rows), jnp.bfloat16),
            pltpu.VMEM((PASSES, 5, 2, 2, cols, rows), jnp.bfloat16),
            pltpu.VMEM((2 * rows, 2 * half), jnp.bfloat16),
            pltpu.VMEM((2, NSUB, 1, rows), jnp.float32),
            pltpu.VMEM((FROWS * NSUB * cols, 2 * max(half, rows)), jnp.bfloat16),
            pltpu.VMEM((FROWS * NSUB * cols, 2 * max(half, rows)), jnp.float32),
            pltpu.VMEM(weights.shape, jnp.float32),
            pltpu.VMEM(visibilities.shape, jnp.float32),
            pltpu.VMEM(weights.shape, jnp.float32),
            pltpu.VMEM(exchanged, jnp.bfloat16),
            pltpu.VMEM(exchanged, jnp.bfloat16),
            pltpu.VMEM(exchanged, jnp.bfloat16),
            pltpu.VMEM((FROWS, 2, cols, rows), jnp.float32),
            pltpu.VMEM((PASSES, FROWS, 2, cols, rows), jnp.bfloat16),
            dma((PASSES, 2, 3)), dma((PASSES, 2, 3)), dma((PASSES, 9)), dma((PASSES, 5, 2)), dma((2,)), dma((2,)),
            dma((PASSES, ns)), dma((PASSES, ns)), dma((PASSES, ns)), dma((PASSES, ns)),
            dma((PASSES, 9)), dma((PASSES, 6)), dma((PASSES, nf)), dma((PASSES,)), dma((5,)),
        ],
        cost_estimate=pl.CostEstimate(flops=flops, bytes_accessed=4 * facets.size, transcendentals=0),
        compiler_params=pltpu.CompilerParams(
            collective_id=0, has_side_effects=True, vmem_limit_bytes=50 * 1024 * 1024),
    )(*(pltpu.with_memory_space_constraint(value, pltpu.HBM) for value in (facets, offsets, visibilities, weights, mask)))


def solution(mesh):
    placed = (
        P("facet", None, None, "strip"),
        P(),
        P(None, "strip", "facet"),
        P("strip", "facet"),
        P("strip", "facet"),
    )
    return jax.shard_map(
        functools.partial(on_device, mesh.shape["facet"], mesh.shape["strip"]),
        mesh=mesh,
        in_specs=placed,
        out_specs=P("facet", None, None, "strip"),
        check_vma=False,
    )
```

```python
import functools
import math

import jax
import jax.numpy as jnp
from jax import lax
from jax.experimental import pallas as pl
from jax.experimental.pallas import tpu as pltpu
from jax.sharding import PartitionSpec as P

NSUB = 4
FROWS = 4
MESH = pl.DeviceIdType.MESH


def turn(count, cells):
    quarter = cells // 4
    shift = quarter.bit_length() - 1
    quadrant = (count + quarter // 2) >> shift
    angle = (count - (quadrant << shift)).astype(jnp.float32) * (2.0 * math.pi / cells)
    square = angle * angle
    sine = angle * (1.0 + square * (-1.0 / 6 + square * (1.0 / 120 + square * (-1.0 / 5040 + square * (1.0 / 362880)))))
    cosine = 1.0 + square * (-0.5 + square * (1.0 / 24 + square * (-1.0 / 720 + square * (1.0 / 40320))))
    odd = (quadrant & 1) == 1
    first = jnp.where(odd, sine, cosine)
    second = jnp.where(odd, cosine, sine)
    cos_value = jnp.where(((quadrant + 1) & 2) == 2, -first, first)
    sin_value = jnp.where((quadrant & 2) == 2, -second, second)
    return cos_value, sin_value


def quarter_turn(count):
    part = count & 3
    sign = jnp.where(part >= 2, -1.0, 1.0)
    even = (part & 1) == 0
    return jnp.where(even, sign, 0.0), jnp.where(even, 0.0, sign)


PASSES = 2


def kernel(
    nf, ns,
    facets, offsets_in, vis, weights_in, mask_in, out,
    offsets, weights, mask, mine, relayed, joint, parts, table, phase, lhs, acc, factor, vis_here, factor_here, partial, partials, resid, sums, update,
    r_send, r_recv, a_send, a_recv, v_send, v_recv, c_send, c_recv, e_send, e_recv, g_send, f_send, g_recv, g_local, local_sem,
):
    f = lax.axis_index("facet")
    t = lax.axis_index("strip")
    cols, rows = parts.shape[4], parts.shape[5]
    cells = FROWS * rows * ns
    half = table.shape[1] // 2
    chunk = partial.shape[4]
    chunks = half // chunk
    scale = 1.0 / math.sqrt(rows * ns)
    start = t * rows
    apart = f != t

    depth = nf // 2
    z = lax.div(f, 2)
    x = lax.rem(f, 2)
    odd = lax.rem(z, 2)

    def facet_at(dz, side):
        return lax.rem(z + dz + depth, depth) * 2 + side

    def strip_peer(i):
        return lax.rem(t + i, ns)

    def columns_of(g, p):
        return pl.ds(pl.multiple_of((g * PASSES + p) * cols, cols), cols)

    barrier = pltpu.get_barrier_semaphore()

    def greet_strip(i, _):
        pl.semaphore_signal(barrier, inc=1, device_id=(f, strip_peer(i)), device_id_type=MESH)
        return 0

    for dz in (1, -1, 2, -2):
        for side in range(2):
            pl.semaphore_signal(barrier, inc=1, device_id=(facet_at(dz, side), t), device_id_type=MESH)
    pl.semaphore_signal(barrier, inc=1, device_id=(facet_at(0, 1 - x), t), device_id_type=MESH)
    lax.fori_loop(1, ns, greet_strip, 0)

    @pl.when(apart)
    def _():
        pl.semaphore_signal(barrier, inc=1, device_id=(t, f), device_id_type=MESH)

    get_offsets = pltpu.make_async_copy(offsets_in, offsets, local_sem.at[0])
    get_weights = pltpu.make_async_copy(weights_in, weights, local_sem.at[1])
    get_mask = pltpu.make_async_copy(mask_in, mask, local_sem.at[2])
    get_vis = pltpu.make_async_copy(vis, vis_here, local_sem.at[3])
    get_offsets.start()
    get_weights.start()
    get_mask.start()
    get_mine = pltpu.make_async_copy(facets.at[0], mine, local_sem.at[4])
    get_mine.start()

    pl.semaphore_wait(barrier, 9 + ns - 1 + apart.astype(jnp.int32))

    routes = (((1, 0), (1, 1), (2, 0)), ((-1, 0), (-1, 1), (-2, 1)))
    place = {1: 0, -1: 1, 2: 2, -2: 3, 0: 4}

    def relay(p, way, u):
        step = 2 - 4 * way
        dz, side = routes[way][u]
        return pltpu.make_async_remote_copy(
            src_ref=mine.at[:, columns_of(facet_at(dz + step, side), p), :], dst_ref=relayed.at[p, way, u],
            send_sem=r_send.at[p, way, u], recv_sem=r_recv.at[p, way, u],
            device_id=(facet_at(step, x), t), device_id_type=MESH)

    def joined(p, way, u):
        dz, side = routes[way][u]
        return pltpu.make_async_remote_copy(
            src_ref=joint.at[p, way, u], dst_ref=parts.at[p, place[dz], x],
            send_sem=a_send.at[p, 3 * way + u], recv_sem=a_recv.at[p, place[dz], x],
            device_id=(facet_at(dz, side), t), device_id_type=MESH)

    def direct(p, n):
        dz, side = ((2, 1), (-2, 0), (0, 1 - x))[n]
        peer = facet_at(dz, side)
        return pltpu.make_async_remote_copy(
            src_ref=mine.at[:, columns_of(peer, p), :], dst_ref=parts.at[p, place[dz], x],
            send_sem=a_send.at[p, 6 + n], recv_sem=a_recv.at[p, place[dz], x],
            device_id=(peer, t), device_id_type=MESH)

    def arrive_part(p, k, side):
        return pltpu.make_async_remote_copy(
            src_ref=parts.at[p, k, side], dst_ref=parts.at[p, k, side],
            send_sem=a_send.at[p, 0], recv_sem=a_recv.at[p, k, side],
            device_id=(facet_at(0, 1 - x), t), device_id_type=MESH)

    def start_relays(p):
        for u in range(3):
            for way in range(2):
                relay(p, way, u).start()
        for n in range(3):
            direct(p, n).start()

    def join(p):
        for u in range(3):
            for way in range(2):
                relay(p, way, u).wait_recv()
                own = mine[:, columns_of(facet_at(*routes[way][u]), p), :]
                joint[p, way, u] = (relayed[p, way, u].astype(jnp.float32) + own.astype(jnp.float32)).astype(jnp.bfloat16)
                joined(p, way, u).start()
                if p + 1 < PASSES:
                    relay(p + 1, way, u).start()

    get_mine.wait()
    start_relays(0)
    for n in range(3):
        direct(1, n).start()
    get_weights.wait()
    get_mask.wait()
    factor[...] = weights[...] * mask[...].astype(jnp.float32)
    send_vis = pltpu.make_async_remote_copy(
        src_ref=vis, dst_ref=vis_here, send_sem=v_send.at[0], recv_sem=v_recv.at[0], device_id=(t, f), device_id_type=MESH)
    send_factor = pltpu.make_async_remote_copy(
        src_ref=factor, dst_ref=factor_here, send_sem=v_send.at[1], recv_sem=v_recv.at[1], device_id=(t, f), device_id_type=MESH)

    @pl.when(jnp.logical_not(apart))
    def _():
        get_vis.start()
        factor_here[...] = factor[...]
        get_vis.wait()

    get_offsets.wait()

    with jax.named_scope("tables"):
        block = min(32, rows)

        def fill(i, _):
            base = pl.multiple_of(i * block, block)
            row = start + base + lax.broadcasted_iota(jnp.int32, (block, half), 0)
            j = lax.broadcasted_iota(jnp.int32, (block, half), 1)
            cos_value, sin_value = turn((row * j) & (cells - 1), cells)
            low = pl.ds(base, block)
            high = pl.ds(pl.multiple_of(rows + base, block), block)
            cos_value = cos_value.astype(jnp.bfloat16)
            table[low, :half] = cos_value
            table[high, half:] = cos_value
            table[low, half:] = (-sin_value).astype(jnp.bfloat16)
            table[high, :half] = sin_value.astype(jnp.bfloat16)
            return 0

        lax.fori_loop(0, rows // block, fill, 0)
        for s in range(NSUB):
            row = start + lax.broadcasted_iota(jnp.int32, (1, rows), 1)
            cos_value, sin_value = turn((row * offsets[s]) & (cells - 1), cells)
            phase[0, s] = cos_value
            phase[1, s] = sin_value

    join(0)

    @pl.when(apart)
    def _():
        send_vis.start()
        send_factor.start()

    join(1)

    def psi(r, s):
        j = lax.broadcasted_iota(jnp.int32, (1, half), 1)
        return quarter_turn((offsets[s] + j) * (r + 2))

    def send_partial(peer, p):
        return pltpu.make_async_remote_copy(
            src_ref=partial.at[p, peer], dst_ref=partials.at[p, t],
            send_sem=c_send.at[p, peer], recv_sem=c_recv.at[p, t], device_id=(f, peer), device_id_type=MESH)

    def arrive_partial(peer, p):
        return pltpu.make_async_remote_copy(
            src_ref=partial.at[p, peer], dst_ref=partials.at[p, peer],
            send_sem=c_send.at[p, peer], recv_sem=c_recv.at[p, peer], device_id=(f, peer), device_id_type=MESH)

    def send_resid(peer, p):
        return pltpu.make_async_remote_copy(
            src_ref=resid.at[p, t], dst_ref=resid.at[p, t],
            send_sem=e_send.at[p, peer], recv_sem=e_recv.at[p, t], device_id=(f, peer), device_id_type=MESH)

    def arrive_resid(peer, p):
        return pltpu.make_async_remote_copy(
            src_ref=resid.at[p, peer], dst_ref=resid.at[p, peer],
            send_sem=e_send.at[p, peer], recv_sem=e_recv.at[p, peer], device_id=(f, peer), device_id_type=MESH)

    spread = ((1, 0), (1, 1), (-1, 0), (-1, 1), (2, 0), (2, 1), (-2, 0), (-2, 1), (0, 1 - x))
    passed = ((-1, 0, 2), (1, 0, -2), (-1, 1, 2), (1, 1, -2), (-2, 0, 2), (2, 1, -2))

    def residue_at(dz, side):
        return lax.rem(odd + dz + 2, 2) * 2 + side

    def slot_of(dz, side):
        return (0 if dz in (1, -1) else 2) + side

    def send_update(p, n):
        dz, side = spread[n]
        return pltpu.make_async_remote_copy(
            src_ref=update.at[p, slot_of(dz, side)], dst_ref=out.at[0, :, columns_of(f, p), :],
            send_sem=g_send.at[p, n], recv_sem=g_recv.at[p, f],
            device_id=(facet_at(dz, side), t), device_id_type=MESH)

    def pass_on(p, n):
        dz, side, step = passed[n]
        block = out.at[0, :, columns_of(facet_at(dz, side), p), :]
        return pltpu.make_async_remote_copy(
            src_ref=block, dst_ref=block,
            send_sem=f_send.at[p, n], recv_sem=g_recv.at[p, facet_at(dz, side)],
            device_id=(facet_at(step, x), t), device_id_type=MESH)

    def own_update(p):
        return pltpu.make_async_copy(update.at[p, slot_of(0, x)], out.at[0, :, columns_of(f, p), :], g_local.at[p])

    def arrive_update(p, peer):
        return pltpu.make_async_remote_copy(
            src_ref=update.at[p, 0], dst_ref=out.at[0, :, columns_of(peer, p), :],
            send_sem=g_send.at[p, 0], recv_sem=g_recv.at[p, peer],
            device_id=(facet_at(0, 1 - x), t), device_id_type=MESH)

    def relay_updates(p):
        for n in range(6):
            dz, side, _ = passed[n]
            arrive_update(p, facet_at(dz, side)).wait_recv()
            pass_on(p, n).start()

    def forward(p):
        for k in range(4):
            for side in range(2):
                arrive_part(p, k, side).wait_recv()
        arrive_part(p, 4, 1 - x).wait_recv()
        parts[p, 4, x] = mine[:, columns_of(f, p), :]
        for side in range(2):
            same = residue_at(0, side)
            other = residue_at(1, side)
            two = parts[p, 2, side].astype(jnp.float32) + parts[p, 3, side].astype(jnp.float32)
            sums[same] = two + parts[p, 4, side].astype(jnp.float32)
            sums[other] = parts[p, 0, side].astype(jnp.float32) + parts[p, 1, side].astype(jnp.float32)
        for s in range(NSUB):
            cos_phi = phase[0, s]
            sin_phi = phase[1, s]
            for r in range(FROWS):
                a = sums[r, 0]
                b = sums[r, 1]
                row = (s * FROWS + r) * cols
                lhs[row:row + cols, :rows] = (a * cos_phi + b * sin_phi).astype(jnp.bfloat16)
                lhs[row:row + cols, rows:] = (b * cos_phi - a * sin_phi).astype(jnp.bfloat16)
        acc[...] = jnp.dot(lhs[...], table[...], preferred_element_type=jnp.float32)
        for s in range(NSUB):
            total_re = jnp.zeros((cols, half), jnp.float32)
            total_im = jnp.zeros((cols, half), jnp.float32)
            for r in range(FROWS):
                cos_psi, sin_psi = psi(r, s)
                row = (s * FROWS + r) * cols
                re = acc[row:row + cols, :half]
                im = acc[row:row + cols, half:]
                total_re = total_re + re * cos_psi + im * sin_psi
                total_im = total_im + im * cos_psi - re * sin_psi
            total_re = (total_re * scale).astype(jnp.bfloat16)
            total_im = (total_im * scale).astype(jnp.bfloat16)
            for q in range(chunks):
                peer = s * chunks + q
                partial[p, peer, 0] = total_re[:, q * chunk:(q + 1) * chunk]
                partial[p, peer, 1] = total_im[:, q * chunk:(q + 1) * chunk]

                @pl.when(peer != t)
                def _():
                    send_partial(peer, p).start()

    def weigh(p):
        if p == 0:
            @pl.when(apart)
            def _():
                send_vis.wait_recv()
                send_factor.wait_recv()

        def add_partial(i, total):
            peer = strip_peer(i)
            arrive_partial(peer, p).wait_recv()
            return total + partials[p, peer].astype(jnp.float32)

        model = lax.fori_loop(1, ns, add_partial, partial[p, t].astype(jnp.float32))
        mine = slice(p * cols, (p + 1) * cols)
        resid[p, t] = (factor_here[mine][None] * (vis_here[:, mine] - model)).astype(jnp.bfloat16)

        def start_resid(i, _):
            send_resid(strip_peer(i), p).start()
            return 0

        lax.fori_loop(1, ns, start_resid, 0)

    def adjoint(p):
        def wait_resid(i, _):
            arrive_resid(strip_peer(i), p).wait_recv()
            return 0

        lax.fori_loop(1, ns, wait_resid, 0)
        for r in range(FROWS):
            for s in range(NSUB):
                cos_psi, sin_psi = psi(residue_at(1 - r // 2, r % 2), s)
                row = (r * NSUB + s) * cols
                for q in range(chunks):
                    g = resid[p, s * chunks + q, 0].astype(jnp.float32)
                    h = resid[p, s * chunks + q, 1].astype(jnp.float32)
                    c = cos_psi[:, q * chunk:(q + 1) * chunk]
                    d = sin_psi[:, q * chunk:(q + 1) * chunk]
                    lhs[row:row + cols, q * chunk:(q + 1) * chunk] = (g * c - h * d).astype(jnp.bfloat16)
                    lhs[row:row + cols, half + q * chunk:half + (q + 1) * chunk] = (h * c + g * d).astype(jnp.bfloat16)
        acc[...] = lax.dot_general(
            lhs[...], table[...], (((1,), (1,)), ((), ())), preferred_element_type=jnp.float32)
        for r in range(FROWS):
            total_re = jnp.zeros((cols, rows), jnp.float32)
            total_im = jnp.zeros((cols, rows), jnp.float32)
            for s in range(NSUB):
                cos_phi = phase[0, s]
                sin_phi = phase[1, s]
                row = (r * NSUB + s) * cols
                a = acc[row:row + cols, :rows]
                b = acc[row:row + cols, rows:]
                total_re = total_re + a * cos_phi - b * sin_phi
                total_im = total_im + b * cos_phi + a * sin_phi
            update[p, r, 0] = (total_re * scale).astype(jnp.bfloat16)
            update[p, r, 1] = (total_im * scale).astype(jnp.bfloat16)
            for n in ((0, 2), (1, 3), (4, 6), (5, 7))[r]:
                send_update(p, n).start()

        send_update(p, 8).start()
        own_update(p).start()

    with jax.named_scope("transforms"):
        forward(0)
        weigh(0)
        forward(1)
        adjoint(0)
        weigh(1)
        relay_updates(0)
        adjoint(1)
        relay_updates(1)

    with jax.named_scope("drain"):
        for p in range(PASSES):
            def drain_strip(i, _):
                peer = strip_peer(i)
                send_partial(peer, p).wait_send()
                send_resid(peer, p).wait_send()
                return 0

            lax.fori_loop(1, ns, drain_strip, 0)
            for u in range(3):
                for way in range(2):
                    relay(p, way, u).wait_send()
                    joined(p, way, u).wait_send()
                direct(p, u).wait_send()
            for n in range(9):
                send_update(p, n).wait_send()
            for n in range(6):
                pass_on(p, n).wait_send()
            own_update(p).wait()
            arrive_update(p, facet_at(0, 1 - x)).wait_recv()
            for dz, side in ((-2, 1), (2, 0), (3, 0), (3, 1), (-3, 0), (-3, 1), (4, 0), (4, 1)):
                arrive_update(p, facet_at(dz, side)).wait_recv()

        @pl.when(apart)
        def _():
            send_vis.wait_send()
            send_factor.wait_send()


def on_device(nf, ns, facets, offsets, visibilities, weights, mask):
    _, _, columns, rows = facets.shape
    cols = columns // nf // PASSES
    frequencies = visibilities.shape[2] * nf
    half = frequencies // NSUB
    chunk = frequencies // ns
    hbm = pl.BlockSpec(memory_space=pltpu.HBM)
    dma = pltpu.SemaphoreType.DMA
    flops = 2 * 2 * FROWS * NSUB * cols * PASSES * (2 * rows) * (2 * half)
    exchanged = (PASSES, ns, 2, cols, chunk)
    return pl.pallas_call(
        functools.partial(kernel, nf, ns),
        out_shape=jax.ShapeDtypeStruct(facets.shape, jnp.bfloat16),
        in_specs=[hbm] * 5,
        out_specs=hbm,
        scratch_shapes=[
            pltpu.SMEM(offsets.shape, jnp.int32),
            pltpu.VMEM(weights.shape, jnp.float32),
            pltpu.VMEM(mask.shape, jnp.int32),
            pltpu.VMEM((2, columns, rows), jnp.bfloat16),
            pltpu.VMEM((PASSES, 2, 3, 2, cols, rows), jnp.bfloat16),
            pltpu.VMEM((PASSES, 2, 3, 2, cols, rows), jnp.bfloat16),
            pltpu.VMEM((PASSES, 5, 2, 2, cols, rows), jnp.bfloat16),
            pltpu.VMEM((2 * rows, 2 * half), jnp.bfloat16),
            pltpu.VMEM((2, NSUB, 1, rows), jnp.float32),
            pltpu.VMEM((FROWS * NSUB * cols, 2 * max(half, rows)), jnp.bfloat16),
            pltpu.VMEM((FROWS * NSUB * cols, 2 * max(half, rows)), jnp.float32),
            pltpu.VMEM(weights.shape, jnp.float32),
            pltpu.VMEM(visibilities.shape, jnp.float32),
            pltpu.VMEM(weights.shape, jnp.float32),
            pltpu.VMEM(exchanged, jnp.bfloat16),
            pltpu.VMEM(exchanged, jnp.bfloat16),
            pltpu.VMEM(exchanged, jnp.bfloat16),
            pltpu.VMEM((FROWS, 2, cols, rows), jnp.float32),
            pltpu.VMEM((PASSES, FROWS, 2, cols, rows), jnp.bfloat16),
            dma((PASSES, 2, 3)), dma((PASSES, 2, 3)), dma((PASSES, 9)), dma((PASSES, 5, 2)), dma((2,)), dma((2,)),
            dma((PASSES, ns)), dma((PASSES, ns)), dma((PASSES, ns)), dma((PASSES, ns)),
            dma((PASSES, 9)), dma((PASSES, 6)), dma((PASSES, nf)), dma((PASSES,)), dma((5,)),
        ],
        cost_estimate=pl.CostEstimate(flops=flops, bytes_accessed=4 * facets.size, transcendentals=0),
        compiler_params=pltpu.CompilerParams(
            collective_id=0, has_side_effects=True, vmem_limit_bytes=50 * 1024 * 1024),
    )(*(pltpu.with_memory_space_constraint(value, pltpu.HBM) for value in (facets, offsets, visibilities, weights, mask)))


def solution(mesh):
    placed = (
        P("facet", None, None, "strip"),
        P(),
        P(None, "strip", "facet"),
        P("strip", "facet"),
        P("strip", "facet"),
    )
    return jax.shard_map(
        functools.partial(on_device, mesh.shape["facet"], mesh.shape["strip"]),
        mesh=mesh,
        in_specs=placed,
        out_specs=P("facet", None, None, "strip"),
        check_vma=False,
    )
```
